32 devices in a mesh: kx: 2 (over core), ky: 4 (over y, x), kz: 4 (over z).
Axes of the slice: x: 2, y: 2, z: 4, core: 2. Of those that a mesh axis runs over, the one named last changes fastest.
Arguments:
- populations: float32 [16, 8, 4, 64, 64], P('kx', None, None, 'ky', 'kz'), may hold values from -6 to 6
- force: float32 [16, 3, 4, 64, 64], P('kx', None, None, 'ky', 'kz'), may hold values from -3 to 3
- rate: float32 [16, 4, 64, 64], P('kx', None, 'ky', 'kz'), may hold values from 0.05 to 0.5
- tiles: bfloat16 [4, 1024, 1024], replicated, may hold values from -0.1875 to 0.1875
- send_planes: int32 [2, 4, 4, 4, 2], P('kx', 'ky', 'kz'), may hold values from 0 to 7
- recv_target: int32 [2, 4, 4, 4, 2], P('kx', 'ky', 'kz'), may hold values from 0 to 7
- recv_tile: int32 [2, 4, 4, 4, 2], P('kx', 'ky', 'kz'), may hold values from 0 to 3
- recv_count: int32 [2, 4, 4, 4], P('kx', 'ky', 'kz'), may hold values from 0 to 2, as said below
Outputs:
- final_populations: float32 [16, 8, 4, 64, 64], P('kx', None, None, 'ky', 'kz')
The draws below stay inside these ranges and needn't reach their ends.
Inputs may be any that keep to these rules, and one draw needn't show every extreme that they name: `recv_count`: every receiving brick has some source brick with all 2 slots valid, and some receiving brick has all 2 slots valid from every source brick.
All inputs are finite; a program needn't handle non-finite values.
Results may differ from the reference program's by a relative error of at most 0.0042.
Values may be sent and summed in bfloat16 or wider, within the bound.
A program may use at most 128 MiB of HBM per device.

```python
import math
from functools import partial
import jax
import jax.numpy as jnp
from jax import lax

DRIVES = 8
BANDS = 4
BX = 8
BY = 16
BZ = 16
NT = 4
CAP = 2
ITERS = 2
BRICKS_X = 2
BRICKS_Y = 4
PEERS = 4
KB = 1024
NX = 16
NY = 64
NZ = 64


def draw_recv_count(key, part):
    first_key, second_key, third_key = jax.random.split(key, 3)
    shape_all = (BRICKS_X, BRICKS_Y, PEERS, PEERS)
    counts = jax.random.randint(first_key, shape_all, 0, CAP + 1)
    full_source = jax.random.randint(second_key, (BRICKS_X, BRICKS_Y, PEERS, 1), 0, PEERS)
    column = lax.broadcasted_iota(jnp.int32, shape_all, 3)
    counts = jnp.where(column == full_source, CAP, counts)
    receiver = jax.random.randint(third_key, (), 0, BRICKS_X * BRICKS_Y * PEERS)
    brick_ids = (lax.broadcasted_iota(jnp.int32, shape_all, 0) * BRICKS_Y + lax.broadcasted_iota(jnp.int32, shape_all, 1)) * PEERS + lax.broadcasted_iota(jnp.int32, shape_all, 2)
    counts = jnp.where(brick_ids == receiver, CAP, counts)
    return counts.astype(jnp.int32)


def touch_ends(values, stream_key, least, top_value):
    spot = [jax.random.randint(jax.random.fold_in(stream_key, axis), (), 0, length) for axis, length in enumerate(values.shape)]
    longest = values.shape.index(max(values.shape))
    neighbour = spot[:longest] + [(spot[longest] + 1) % values.shape[longest]] + spot[longest + 1:]
    return values.at[tuple(spot)].set(least).at[tuple(neighbour)].set(top_value)


def levels(rng, extent, pieces, least, largest):
    gain = 1.0
    for dim, blocks in pieces:
        heights = jax.random.uniform(jax.random.fold_in(jax.random.fold_in(rng, 6), dim), (blocks,), jnp.float32, least / len(pieces), largest / len(pieces))
        gain = gain * jnp.repeat(jnp.exp(heights), extent[dim] // blocks).reshape((-1,) + (1,) * (len(extent) - 1 - dim))
    return gain


def normal_values(key, dims, spread, most, pieces=(), kind=jnp.bfloat16):
    entries = jax.random.normal(key, dims, jnp.float32) * spread
    if len(pieces) > 0:
        entries = levels(key, dims, pieces, -0.22, 0.18) * entries
    return jnp.clip(entries, min=-most, max=most).astype(kind)


def setup_inputs(seed: int = 0) -> dict:
    splits = jax.random.split(jax.random.key(seed), 9)
    populations = normal_values(splits[0], (NX, DRIVES, BANDS, NY, NZ), 1.0, 6.0, ((0, 2), (3, 4), (4, 4)), jnp.float32)
    force = normal_values(splits[1], (NX, 3, BANDS, NY, NZ), 0.5, 3.0, ((0, 2), (3, 4), (4, 4)), jnp.float32)
    rate = jnp.clip(jnp.exp(math.log(0.5) - 2.3025851 * jax.random.uniform(splits[2], (NX, BANDS, NY, NZ), jnp.float32) ** levels(splits[2], (NX, BANDS, NY, NZ), ((0, 2), (2, 4), (3, 4)), -0.2, 0.2)), 0.05, 0.5)
    tiles = normal_values(splits[3], (NT, KB, KB), KB ** -0.5, 0.1875)
    send_planes = touch_ends(jax.random.randint(splits[4], (BRICKS_X, BRICKS_Y, PEERS, PEERS, CAP), 0, BX), jax.random.fold_in(splits[4], 1), 0, BX - 1).astype(jnp.int32)
    recv_target = touch_ends(jax.random.randint(splits[5], (BRICKS_X, BRICKS_Y, PEERS, PEERS, CAP), 0, BX), jax.random.fold_in(splits[5], 1), 0, BX - 1).astype(jnp.int32)
    recv_tile = touch_ends(jax.random.randint(splits[6], (BRICKS_X, BRICKS_Y, PEERS, PEERS, CAP), 0, NT), jax.random.fold_in(splits[6], 1), 0, NT - 1).astype(jnp.int32)
    recv_count = draw_recv_count(jax.random.fold_in(splits[8], 71), 0)
    return dict(populations=populations, force=force, rate=rate, tiles=tiles, send_planes=send_planes, recv_target=recv_target, recv_tile=recv_tile, recv_count=recv_count)


def derivative(values, along):
    ahead_one = jnp.roll(values, -1, along)
    behind_one = jnp.roll(values, 1, along)
    ahead_two = jnp.roll(values, -2, along)
    behind_two = jnp.roll(values, 2, along)
    return (8.0 * (ahead_one - behind_one) - (ahead_two - behind_two)) / 12.0


def brick_collision(tiles_wide, inputs):
    received, slot_count, target_ids, tile_ids = inputs
    usable = jnp.arange(CAP, dtype=jnp.int32)[None, :] < slot_count[:, None]
    tile_match = tile_ids[None, :, :] == jnp.arange(NT, dtype=jnp.int32)[:, None, None]
    plane_match = target_ids[None, :, :] == jnp.arange(BX, dtype=jnp.int32)[:, None, None]
    selector = (tile_match[:, None] & plane_match[None] & usable[None, None]).astype(jnp.float32)
    grouped = jnp.einsum("tjpc,pcdk->tjdk", selector, received.astype(jnp.float32)).astype(jnp.bfloat16)
    return jnp.einsum("tjdk,tlk->jdl", grouped.astype(jnp.float32), tiles_wide)


def reference(populations, force, rate, tiles, send_planes, recv_target, recv_tile, recv_count):
    tiles_wide = tiles.astype(jnp.float32)
    bricks = BRICKS_X * BRICKS_Y * PEERS
    current = populations
    for iteration in range(ITERS):
        drift_term = force[:, 0][:, None] * derivative(current, 0)
        drift_term = drift_term + force[:, 1][:, None] * derivative(current, 3)
        drift_term = drift_term + force[:, 2][:, None] * derivative(current, 4)
        rounded = current.astype(jnp.bfloat16)
        planes = rounded.reshape(BRICKS_X, BX, DRIVES, BANDS, BRICKS_Y, BY, PEERS, BZ)
        planes = planes.transpose(0, 4, 6, 1, 2, 3, 5, 7).reshape(BRICKS_X, BRICKS_Y, PEERS, BX, DRIVES, KB)
        chosen = send_planes.reshape(BRICKS_X, BRICKS_Y, PEERS, PEERS * CAP).astype(jnp.int32)[:, :, :, :, None, None]
        sent = jnp.take_along_axis(planes, chosen, axis=3)
        received = sent.reshape(BRICKS_X, BRICKS_Y, PEERS, PEERS, CAP, DRIVES, KB).swapaxes(2, 3)
        received = received.reshape(bricks, PEERS, CAP, DRIVES, KB)
        collision = lax.map(partial(brick_collision, tiles_wide), (received, recv_count.reshape(bricks, PEERS), recv_target.reshape(bricks, PEERS, CAP), recv_tile.reshape(bricks, PEERS, CAP)))
        collision = collision.reshape(BRICKS_X, BRICKS_Y, PEERS, BX, DRIVES, BANDS, BY, BZ)
        collision = collision.transpose(0, 3, 4, 5, 1, 6, 2, 7).reshape(NX, DRIVES, BANDS, NY, NZ)
        current = current - drift_term + collision - rate[:, None] * current
    return current
```

```python
import functools
import jax
import jax.numpy as jnp
from jax import lax
from jax.experimental import pallas as pl
from jax.experimental.pallas import tpu as pltpu
from jax.sharding import PartitionSpec as P

ITERS = 2
MESH = pl.DeviceIdType.MESH
LANES = 128


def roll(v, by):
    by = by % LANES
    return v if by == 0 else pltpu.roll(v, by, axis=1)


def main_kernel(sizes, pop, force, rate, tiles, send_planes, recv_target, recv_tile, recv_count, out,
                pop_in, force_in, rate_in, tiles_in, ext, mid, field, base, y_out, y_in, z_out, z_in,
                p_out, p_in, in_sem, tile_sem, x_send, x_recv, y_send, y_recv, z_send, z_recv, p_send, p_recv):
    n_x, n_y, n_z, wx, drives, bands, wy, wz, cap, n_tiles = sizes
    rows = bands * wy
    length = rows * wz
    pieces = length // LANES
    per = LANES // wz
    halves = wy // per
    mx, my, mz = lax.axis_index("kx"), lax.axis_index("ky"), lax.axis_index("kz")

    def around(me, size, by):
        return lax.rem(me + (by % size), size)

    barrier = pltpu.get_barrier_semaphore()
    friends = []
    for name, me, size, offsets in (("kx", mx, n_x, {1, n_x - 1}), ("ky", my, n_y, {1, n_y - 1}), ("kz", mz, n_z, set(range(1, n_z)))):
        for by in sorted(offsets):
            friends.append({name: around(me, size, by)})
    for friend in friends:
        pl.semaphore_signal(barrier, inc=1, device_id=friend, device_id_type=MESH)

    loads = [pltpu.make_async_copy(a, b, in_sem.at[i]) for i, (a, b) in enumerate(((pop, pop_in), (force, force_in), (rate, rate_in)))]
    for load in loads:
        load.start()
    tile_loads = [pltpu.make_async_copy(tiles.at[t], tiles_in.at[t], tile_sem.at[t]) for t in range(n_tiles)]
    for load in tile_loads:
        load.start()

    lane = lax.broadcasted_iota(jnp.int32, (8, LANES), 1)
    z_of = lax.rem(lane, wz)

    loads[0].wait()

    def lay_pop(x, carry):
        for v in range(pieces):
            piece = jnp.concatenate(
                [pop_in[pl.ds(x * drives * rows + v * per + i, drives, stride=rows), :] for i in range(per)], axis=1)
            ext[0, x + 2, :, v * LANES:(v + 1) * LANES] = piece
            mid[x, :, v * LANES:(v + 1) * LANES] = piece
        return carry

    lax.fori_loop(0, wx, lay_pop, 0)
    pl.semaphore_wait(barrier, len(friends))

    sel = None
    in_flight = []
    for it in range(ITERS):
        cur = ext.at[it]
        waits_p = []
        for k in range(n_z - 1, -1, -1):
            peer = around(mz, n_z, k)
            blocks = jnp.concatenate(
                [mid[send_planes[0, 0, 0, c, peer]] for c in range(cap)], axis=0).astype(jnp.bfloat16)
            if k == 0:
                p_in[it, 0:cap * drives, :] = blocks
            else:
                p_out[it, k * cap * drives:(k + 1) * cap * drives, :] = blocks
                part = pl.ds(k * cap * drives, cap * drives)
                copy = pltpu.make_async_remote_copy(
                    p_out.at[it, part], p_in.at[it, part], p_send.at[it, k], p_recv.at[it, k],
                    device_id={"kz": peer}, device_id_type=MESH)
                copy.start()
                waits_p.append(copy)
        waits_h = [
            pltpu.make_async_remote_copy(
                cur.at[wx:wx + 2], cur.at[0:2], x_send.at[it, 0], x_recv.at[it, 0],
                device_id={"kx": around(mx, n_x, 1)}, device_id_type=MESH),
            pltpu.make_async_remote_copy(
                cur.at[2:4], cur.at[wx + 2:wx + 4], x_send.at[it, 1], x_recv.at[it, 1],
                device_id={"kx": around(mx, n_x, -1)}, device_id_type=MESH)]
        for copy in waits_h:
            copy.start()

        def pack(x, carry):
            part = [cur[x + 2, :, v * LANES:(v + 1) * LANES] for v in range(pieces)]
            up_z = jnp.zeros((drives, LANES), jnp.float32)
            down_z = up_z
            for v in range(pieces):
                c = part[v]
                last = jnp.where(z_of == wz - 2, c - 8.0 * roll(c, -1), c)
                first = jnp.where(z_of == 0, -c, 8.0 * roll(c, 1) - c)
                here = lax.div(z_of, 2) == v
                up_z = jnp.where(here, roll(last, 2 * v - (wz - 2)), up_z)
                down_z = jnp.where(here, roll(first, 2 * v), down_z)
            z_out[it, 0, x] = up_z
            z_out[it, 1, x] = down_z
            up_y = jnp.zeros((drives, LANES), jnp.float32)
            down_y = up_y
            width = 2 * wz
            for b in range(bands):
                here = lax.div(lane, width) == b
                up_y = jnp.where(here, roll(part[b * halves + halves - 1], width * b - (LANES - width)), up_y)
                down_y = jnp.where(here, roll(part[b * halves], width * b), down_y)
            y_out[it, 0, x] = up_y
            y_out[it, 1, x] = down_y
            return carry

        lax.fori_loop(0, wx, pack, 0)
        for name, me, size, o, i, ss, rs in (("kz", mz, n_z, z_out, z_in, z_send, z_recv), ("ky", my, n_y, y_out, y_in, y_send, y_recv)):
            for way in range(2):
                copy = pltpu.make_async_remote_copy(
                    o.at[it, way], i.at[it, way], ss.at[it, way], rs.at[it, way],
                    device_id={name: around(me, size, 1 if way == 0 else -1)}, device_id_type=MESH)
                copy.start()
                waits_h.append(copy)

        if it == 0:
            loads[1].wait()
            loads[2].wait()
            for v in range(pieces):
                at = slice(v * LANES, (v + 1) * LANES)
                for a in range(4):
                    source, first, stride = (force_in, a * rows, 3 * rows) if a < 3 else (rate_in, 0, rows)
                    piece = jnp.concatenate(
                        [source[pl.ds(first + v * per + i, wx, stride=stride), :] for i in range(per)], axis=1)
                    if a < 3:
                        piece = piece * (1.0 / 12.0)
                    for x in range(wx):
                        field[a, x, :, at] = jnp.broadcast_to(piece[x:x + 1], (drives, LANES))
            slots = n_z * cap
            col = lax.broadcasted_iota(jnp.int32, (8, slots * drives), 1)
            pair = jnp.full((8, slots * drives), -1, jnp.int32)
            for k in range(n_z):
                source = around(mz, n_z, -k)
                count = recv_count[0, 0, 0, source]
                for c in range(cap):
                    code = jnp.where(c < count, recv_tile[0, 0, 0, c, source] * wx + recv_target[0, 0, 0, c, source], -1)
                    pair = jnp.where(lax.div(col, drives) == k * cap + c, code, pair)
            row = lax.broadcasted_iota(jnp.int32, (n_tiles * wx * drives, slots * drives), 0)
            col = lax.broadcasted_iota(jnp.int32, (n_tiles * wx * drives, slots * drives), 1)
            hit = (lax.div(row, drives) == pair[0:1]) & (lax.rem(row, drives) == lax.rem(col, drives))
            sel = jnp.where(hit, 1.0, 0.0).astype(jnp.bfloat16)

        for copy in waits_h:
            copy.wait_recv()

        def step(x, carry):
            zp, zn = z_in[it, 0, x], z_in[it, 1, x]
            yp, yn = y_in[it, 0, x], y_in[it, 1, x]
            width = 2 * wz
            part = [cur[x + 2, :, v * LANES:(v + 1) * LANES] for v in range(pieces)]
            for v in range(pieces):
                at = slice(v * LANES, (v + 1) * LANES)
                b, h = divmod(v, halves)
                c = part[v]
                dx = 8.0 * (cur[x + 3, :, at] - cur[x + 1, :, at]) - (cur[x + 4, :, at] - cur[x, :, at])
                after = part[v + 1] if h < halves - 1 else roll(yn, -width * b)
                before = part[v - 1] if h > 0 else roll(yp, LANES - width - width * b)
                y1 = roll(jnp.where(lane < wz, after, c), -wz)
                y2 = roll(jnp.where(lane < 2 * wz, after, c), -2 * wz)
                w1 = roll(jnp.where(lane >= LANES - wz, before, c), wz)
                w2 = roll(jnp.where(lane >= LANES - 2 * wz, before, c), 2 * wz)
                dy = 8.0 * (y1 - w1) - (y2 - w2)
                a1 = jnp.where(z_of < wz - 1, roll(c, -1), 0.0)
                b1 = jnp.where(z_of >= 1, roll(c, 1), 0.0)
                a2 = jnp.where(z_of < wz - 2, roll(c, -2), 0.0)
                b2 = jnp.where(z_of >= 2, roll(c, 2), 0.0)
                edge = jnp.where(z_of < 2, roll(zp, -2 * v), jnp.where(z_of >= wz - 2, roll(zn, wz - 2 - 2 * v), 0.0))
                dz = 8.0 * (a1 - b1) - (a2 - b2) + edge
                fx, fy, fz, r = (field[a, x, :, at] for a in range(4))
                base[pl.ds(pl.multiple_of(x * drives, drives), drives), at] = c - (fx * dx + fy * dy + fz * dz) - r * c
            return carry

        lax.fori_loop(0, wx, step, 0)

        for copy in waits_p:
            copy.wait_recv()
        grouped = jnp.dot(sel, p_in[it], preferred_element_type=jnp.float32).astype(jnp.bfloat16)
        m = wx * drives
        total = base[...]
        for t in range(n_tiles):
            if it == 0:
                tile_loads[t].wait()
            total = total + lax.dot_general(
                grouped[t * m:(t + 1) * m], tiles_in[t], (((1,), (1,)), ((), ())), preferred_element_type=jnp.float32)
        total = total.reshape(wx, drives, length)
        if it == ITERS - 1:
            out[...] = total
        else:
            ext[it + 1, 2:wx + 2] = total
            mid[...] = total
        in_flight += waits_p + waits_h
    for copy in in_flight:
        copy.wait_send()


def spread_kernel(sizes, dense, out):
    wx, drives, rows, wz = sizes
    per = LANES // wz
    pieces = rows // per

    def lay(x, carry):
        for v in range(pieces):
            piece = dense[x, :, v * LANES:(v + 1) * LANES]
            for i in range(per):
                out[pl.ds(x * drives * rows + v * per + i, drives, stride=rows), :] = roll(piece, -i * wz)[:, :wz]
        return carry

    lax.fori_loop(0, wx, lay, 0)


def per_device(mesh_shape, populations, force, rate, tiles, send_planes, recv_target, recv_tile, recv_count):
    wx, drives, bands, wy, wz = populations.shape
    cap = send_planes.shape[-1]
    n_tiles, length, _ = tiles.shape
    n_x, n_y, n_z = mesh_shape
    rows = bands * wy
    sizes = (n_x, n_y, n_z, wx, drives, bands, wy, wz, cap, n_tiles)
    vmem = pl.BlockSpec(memory_space=pltpu.VMEM)
    smem = pl.BlockSpec(memory_space=pltpu.SMEM)
    anywhere = pl.BlockSpec(memory_space=pl.ANY)
    f32, b16 = jnp.float32, jnp.bfloat16
    dma = pltpu.SemaphoreType.DMA
    dense = pl.pallas_call(
        functools.partial(main_kernel, sizes),
        out_shape=jax.ShapeDtypeStruct((wx, drives, length), f32),
        in_specs=[anywhere] * 4 + [smem] * 4,
        out_specs=vmem,
        scratch_shapes=[
            pltpu.VMEM((wx * drives * rows, wz), f32),
            pltpu.VMEM((wx * 3 * rows, wz), f32),
            pltpu.VMEM((wx * rows, wz), f32),
            pltpu.VMEM(tiles.shape, b16),
            pltpu.VMEM((ITERS, wx + 4, drives, length), f32),
            pltpu.VMEM((wx, drives, length), f32),
            pltpu.VMEM((4, wx, drives, length), f32),
            pltpu.VMEM((wx * drives, length), f32),
            pltpu.VMEM((ITERS, 2, wx, drives, LANES), f32),
            pltpu.VMEM((ITERS, 2, wx, drives, LANES), f32),
            pltpu.VMEM((ITERS, 2, wx, drives, LANES), f32),
            pltpu.VMEM((ITERS, 2, wx, drives, LANES), f32),
            pltpu.VMEM((ITERS, n_z * cap * drives, length), b16),
            pltpu.VMEM((ITERS, n_z * cap * drives, length), b16),
            dma((3,)), dma((n_tiles,)),
            dma((ITERS, 2)), dma((ITERS, 2)), dma((ITERS, 2)), dma((ITERS, 2)), dma((ITERS, 2)), dma((ITERS, 2)),
            dma((ITERS, n_z)), dma((ITERS, n_z)),
        ],
        compiler_params=pltpu.CompilerParams(collective_id=0, has_side_effects=True, vmem_limit_bytes=48 * 2**20),
        name="steps",
    )(
        populations.reshape(wx * drives * rows, wz),
        force.reshape(wx * 3 * rows, wz),
        rate.reshape(wx * rows, wz),
        tiles,
        jnp.swapaxes(send_planes, -1, -2),
        jnp.swapaxes(recv_target, -1, -2),
        jnp.swapaxes(recv_tile, -1, -2),
        recv_count,
    )
    spread = pl.pallas_call(
        functools.partial(spread_kernel, (wx, drives, rows, wz)),
        out_shape=jax.ShapeDtypeStruct((wx * drives * rows, wz), f32),
        in_specs=[vmem],
        out_specs=vmem,
        compiler_params=pltpu.CompilerParams(vmem_limit_bytes=16 * 2**20),
        name="spread",
    )(dense)
    return spread.reshape(populations.shape)


def solution(mesh):
    placed = (
        P("kx", None, None, "ky", "kz"),
        P("kx", None, None, "ky", "kz"),
        P("kx", None, "ky", "kz"),
        P(),
        P("kx", "ky", "kz", None, None),
        P("kx", "ky", "kz", None, None),
        P("kx", "ky", "kz", None, None),
        P("kx", "ky", "kz", None),
    )
    sizes = tuple(mesh.shape[a] for a in ("kx", "ky", "kz"))
    return jax.shard_map(
        functools.partial(per_device, sizes),
        mesh=mesh,
        in_specs=placed,
        out_specs=P("kx", None, None, "ky", "kz"),
        check_vma=False,
    )
```

```python
import functools
import jax
import jax.numpy as jnp
from jax import lax
from jax.experimental import pallas as pl
from jax.experimental.pallas import tpu as pltpu
from jax.sharding import PartitionSpec as P

ITERS = 2
MESH = pl.DeviceIdType.MESH
LANES = 128


def roll(v, by):
    by = by % LANES
    return v if by == 0 else pltpu.roll(v, by, axis=1)


def main_kernel(sizes, pop, force, rate, tiles, send_hbm, target_hbm, tile_hbm, count_hbm, out,
                send_planes, recv_target, recv_tile, recv_count, pop_in, force_in, rate_in, tiles_in, ext, mid, field, base, y_out, y_in, z_out, z_in,
                p_out, p_in, in_sem, pop_sem, tile_sem, x_send, x_recv, y_send, y_recv, z_send, z_recv, p_send, p_recv):
    n_x, n_y, n_z, wx, drives, bands, wy, wz, cap, n_tiles = sizes
    rows = bands * wy
    length = rows * wz
    pieces = length // LANES
    per = LANES // wz
    halves = wy // per
    mx, my, mz = lax.axis_index("kx"), lax.axis_index("ky"), lax.axis_index("kz")

    def around(me, size, by):
        return lax.rem(me + (by % size), size)

    barrier = pltpu.get_barrier_semaphore()
    friends = []
    for name, me, size, offsets in (("kx", mx, n_x, {1, n_x - 1}), ("ky", my, n_y, {1, n_y - 1}), ("kz", mz, n_z, set(range(1, n_z)))):
        for by in sorted(offsets):
            friends.append({name: around(me, size, by)})
    for friend in friends:
        pl.semaphore_signal(barrier, inc=1, device_id=friend, device_id_type=MESH)

    pop_rows = drives * rows
    pop_loads = [pltpu.make_async_copy(pop.at[pl.ds(x * pop_rows, pop_rows)], pop_in.at[pl.ds(x * pop_rows, pop_rows)], pop_sem.at[x])
                 for x in range(wx)]
    for load in pop_loads:
        load.start()
    pairs = ((send_hbm, send_planes), (target_hbm, recv_target), (tile_hbm, recv_tile), (count_hbm, recv_count), (force, force_in), (rate, rate_in))
    loads = [pltpu.make_async_copy(a, b, in_sem.at[i]) for i, (a, b) in enumerate(pairs)]
    for load in loads:
        load.start()
    tile_loads = [pltpu.make_async_copy(tiles.at[t], tiles_in.at[t], tile_sem.at[t]) for t in range(n_tiles)]
    for load in tile_loads:
        load.start()

    lane = lax.broadcasted_iota(jnp.int32, (8, LANES), 1)
    z_of = lax.rem(lane, wz)

    for x in range(wx):
        pop_loads[x].wait()
        for v in range(pieces):
            piece = jnp.concatenate(
                [pop_in[pl.ds(x * pop_rows + v * per + i, drives, stride=rows), :] for i in range(per)], axis=1)
            ext[0, x + 2, :, v * LANES:(v + 1) * LANES] = piece
            mid[x, :, v * LANES:(v + 1) * LANES] = piece
    loads[0].wait()
    pl.semaphore_wait(barrier, len(friends))

    sel = None
    in_flight = []
    for it in range(ITERS):
        cur = ext.at[it]
        waits_p = []
        for k in range(n_z - 1, -1, -1):
            peer = around(mz, n_z, k)
            blocks = jnp.concatenate(
                [mid[send_planes[0, 0, 0, c, peer]] for c in range(cap)], axis=0).astype(jnp.bfloat16)
            if k == 0:
                p_in[it, 0:cap * drives, :] = blocks
            else:
                p_out[it, k * cap * drives:(k + 1) * cap * drives, :] = blocks
                part = pl.ds(k * cap * drives, cap * drives)
                copy = pltpu.make_async_remote_copy(
                    p_out.at[it, part], p_in.at[it, part], p_send.at[it, k], p_recv.at[it, k],
                    device_id={"kz": peer}, device_id_type=MESH)
                copy.start()
                waits_p.append(copy)
        waits_h = [
            pltpu.make_async_remote_copy(
                cur.at[wx:wx + 2], cur.at[0:2], x_send.at[it, 0], x_recv.at[it, 0],
                device_id={"kx": around(mx, n_x, 1)}, device_id_type=MESH),
            pltpu.make_async_remote_copy(
                cur.at[2:4], cur.at[wx + 2:wx + 4], x_send.at[it, 1], x_recv.at[it, 1],
                device_id={"kx": around(mx, n_x, -1)}, device_id_type=MESH)]
        for copy in waits_h:
            copy.start()

        def pack(x, carry):
            part = [cur[x + 2, :, v * LANES:(v + 1) * LANES] for v in range(pieces)]
            up_z = jnp.zeros((drives, LANES), jnp.float32)
            down_z = up_z
            for v in range(pieces):
                c = part[v]
                last = jnp.where(z_of == wz - 2, c - 8.0 * roll(c, -1), c)
                first = jnp.where(z_of == 0, -c, 8.0 * roll(c, 1) - c)
                here = lax.div(z_of, 2) == v
                up_z = jnp.where(here, roll(last, 2 * v - (wz - 2)), up_z)
                down_z = jnp.where(here, roll(first, 2 * v), down_z)
            z_out[it, 0, x] = up_z
            z_out[it, 1, x] = down_z
            up_y = jnp.zeros((drives, LANES), jnp.float32)
            down_y = up_y
            width = 2 * wz
            for b in range(bands):
                here = lax.div(lane, width) == b
                up_y = jnp.where(here, roll(part[b * halves + halves - 1], width * b - (LANES - width)), up_y)
                down_y = jnp.where(here, roll(part[b * halves], width * b), down_y)
            y_out[it, 0, x] = up_y
            y_out[it, 1, x] = down_y
            return carry

        lax.fori_loop(0, wx, pack, 0)
        for name, me, size, o, i, ss, rs in (("kz", mz, n_z, z_out, z_in, z_send, z_recv), ("ky", my, n_y, y_out, y_in, y_send, y_recv)):
            for way in range(2):
                copy = pltpu.make_async_remote_copy(
                    o.at[it, way], i.at[it, way], ss.at[it, way], rs.at[it, way],
                    device_id={name: around(me, size, 1 if way == 0 else -1)}, device_id_type=MESH)
                copy.start()
                waits_h.append(copy)

        if it == 0:
            for load in loads[1:]:
                load.wait()
            for v in range(pieces):
                at = slice(v * LANES, (v + 1) * LANES)
                for a in range(4):
                    source, first, stride = (force_in, a * rows, 3 * rows) if a < 3 else (rate_in, 0, rows)
                    piece = jnp.concatenate(
                        [source[pl.ds(first + v * per + i, wx, stride=stride), :] for i in range(per)], axis=1)
                    if a < 3:
                        piece = piece * (1.0 / 12.0)
                    for x in range(wx):
                        field[a, x, :, at] = jnp.broadcast_to(piece[x:x + 1], (drives, LANES))
            slots = n_z * cap
            col = lax.broadcasted_iota(jnp.int32, (8, slots * drives), 1)
            pair = jnp.full((8, slots * drives), -1, jnp.int32)
            for k in range(n_z):
                source = around(mz, n_z, -k)
                count = recv_count[0, 0, 0, source]
                for c in range(cap):
                    code = jnp.where(c < count, recv_tile[0, 0, 0, c, source] * wx + recv_target[0, 0, 0, c, source], -1)
                    pair = jnp.where(lax.div(col, drives) == k * cap + c, code, pair)
            row = lax.broadcasted_iota(jnp.int32, (n_tiles * wx * drives, slots * drives), 0)
            col = lax.broadcasted_iota(jnp.int32, (n_tiles * wx * drives, slots * drives), 1)
            hit = (lax.div(row, drives) == pair[0:1]) & (lax.rem(row, drives) == lax.rem(col, drives))
            sel = jnp.where(hit, 1.0, 0.0).astype(jnp.bfloat16)

        for copy in waits_h:
            copy.wait_recv()

        def step(x, carry):
            zp, zn = z_in[it, 0, x], z_in[it, 1, x]
            yp, yn = y_in[it, 0, x], y_in[it, 1, x]
            width = 2 * wz
            part = [cur[x + 2, :, v * LANES:(v + 1) * LANES] for v in range(pieces)]
            for v in range(pieces):
                at = slice(v * LANES, (v + 1) * LANES)
                b, h = divmod(v, halves)
                c = part[v]
                dx = 8.0 * (cur[x + 3, :, at] - cur[x + 1, :, at]) - (cur[x + 4, :, at] - cur[x, :, at])
                after = part[v + 1] if h < halves - 1 else roll(yn, -width * b)
                before = part[v - 1] if h > 0 else roll(yp, LANES - width - width * b)
                y1 = roll(jnp.where(lane < wz, after, c), -wz)
                y2 = roll(jnp.where(lane < 2 * wz, after, c), -2 * wz)
                w1 = roll(jnp.where(lane >= LANES - wz, before, c), wz)
                w2 = roll(jnp.where(lane >= LANES - 2 * wz, before, c), 2 * wz)
                dy = 8.0 * (y1 - w1) - (y2 - w2)
                a1 = jnp.where(z_of < wz - 1, roll(c, -1), 0.0)
                b1 = jnp.where(z_of >= 1, roll(c, 1), 0.0)
                a2 = jnp.where(z_of < wz - 2, roll(c, -2), 0.0)
                b2 = jnp.where(z_of >= 2, roll(c, 2), 0.0)
                edge = jnp.where(z_of < 2, roll(zp, -2 * v), jnp.where(z_of >= wz - 2, roll(zn, wz - 2 - 2 * v), 0.0))
                dz = 8.0 * (a1 - b1) - (a2 - b2) + edge
                fx, fy, fz, r = (field[a, x, :, at] for a in range(4))
                base[pl.ds(pl.multiple_of(x * drives, drives), drives), at] = c - (fx * dx + fy * dy + fz * dz) - r * c
            return carry

        lax.fori_loop(0, wx, step, 0)

        for copy in waits_p:
            copy.wait_recv()
        grouped = jnp.dot(sel, p_in[it], preferred_element_type=jnp.float32).astype(jnp.bfloat16)
        m = wx * drives
        total = base[...]
        for t in range(n_tiles):
            if it == 0:
                tile_loads[t].wait()
            total = total + lax.dot_general(
                grouped[t * m:(t + 1) * m], tiles_in[t], (((1,), (1,)), ((), ())), preferred_element_type=jnp.float32)
        total = total.reshape(wx, drives, length)
        if it == ITERS - 1:
            out[...] = total
        else:
            ext[it + 1, 2:wx + 2] = total
            mid[...] = total
        in_flight += waits_p + waits_h
    for copy in in_flight:
        copy.wait_send()


def spread_kernel(sizes, dense_hbm, out, dense, laid, in_sem, sem):
    wx, drives, rows, wz = sizes
    per = LANES // wz
    pieces = rows // per
    loads = [pltpu.make_async_copy(dense_hbm.at[x], dense.at[x], in_sem.at[x]) for x in range(wx)]
    for load in loads:
        load.start()
    copies = []
    for x in range(wx):
        loads[x].wait()
        for v in range(pieces):
            piece = dense[x, :, v * LANES:(v + 1) * LANES]
            for i in range(per):
                laid[pl.ds(x * drives * rows + v * per + i, drives, stride=rows), :] = roll(piece, -i * wz)[:, :wz]
        part = pl.ds(x * drives * rows, drives * rows)
        copies.append(pltpu.make_async_copy(laid.at[part], out.at[part], sem.at[x]))
        copies[-1].start()
    for copy in copies:
        copy.wait()


def per_device(mesh_shape, populations, force, rate, tiles, send_planes, recv_target, recv_tile, recv_count):
    wx, drives, bands, wy, wz = populations.shape
    cap = send_planes.shape[-1]
    n_tiles, length, _ = tiles.shape
    n_x, n_y, n_z = mesh_shape
    rows = bands * wy
    sizes = (n_x, n_y, n_z, wx, drives, bands, wy, wz, cap, n_tiles)
    vmem = pl.BlockSpec(memory_space=pltpu.VMEM)
    hbm = pl.BlockSpec(memory_space=pltpu.HBM)
    f32, b16 = jnp.float32, jnp.bfloat16
    dma = pltpu.SemaphoreType.DMA
    dense = pl.pallas_call(
        functools.partial(main_kernel, sizes),
        out_shape=jax.ShapeDtypeStruct((wx, drives, length), f32),
        in_specs=[hbm] * 8,
        out_specs=vmem,
        scratch_shapes=[
            pltpu.SMEM((1, 1, 1, cap, n_z), jnp.int32),
            pltpu.SMEM((1, 1, 1, cap, n_z), jnp.int32),
            pltpu.SMEM((1, 1, 1, cap, n_z), jnp.int32),
            pltpu.SMEM((1, 1, 1, n_z), jnp.int32),
            pltpu.VMEM((wx * drives * rows, wz), f32),
            pltpu.VMEM((wx * 3 * rows, wz), f32),
            pltpu.VMEM((wx * rows, wz), f32),
            pltpu.VMEM(tiles.shape, b16),
            pltpu.VMEM((ITERS, wx + 4, drives, length), f32),
            pltpu.VMEM((wx, drives, length), f32),
            pltpu.VMEM((4, wx, drives, length), f32),
            pltpu.VMEM((wx * drives, length), f32),
            pltpu.VMEM((ITERS, 2, wx, drives, LANES), f32),
            pltpu.VMEM((ITERS, 2, wx, drives, LANES), f32),
            pltpu.VMEM((ITERS, 2, wx, drives, LANES), f32),
            pltpu.VMEM((ITERS, 2, wx, drives, LANES), f32),
            pltpu.VMEM((ITERS, n_z * cap * drives, length), b16),
            pltpu.VMEM((ITERS, n_z * cap * drives, length), b16),
            dma((6,)), dma((wx,)), dma((n_tiles,)),
            dma((ITERS, 2)), dma((ITERS, 2)), dma((ITERS, 2)), dma((ITERS, 2)), dma((ITERS, 2)), dma((ITERS, 2)),
            dma((ITERS, n_z)), dma((ITERS, n_z)),
        ],
        compiler_params=pltpu.CompilerParams(collective_id=0, has_side_effects=True, vmem_limit_bytes=60 * 2**20),
        name="steps",
    )(
        populations.reshape(wx * drives * rows, wz),
        force.reshape(wx * 3 * rows, wz),
        rate.reshape(wx * rows, wz),
        tiles,
        jnp.swapaxes(send_planes, -1, -2),
        jnp.swapaxes(recv_target, -1, -2),
        jnp.swapaxes(recv_tile, -1, -2),
        recv_count,
    )
    spread = pl.pallas_call(
        functools.partial(spread_kernel, (wx, drives, rows, wz)),
        out_shape=jax.ShapeDtypeStruct((wx * drives * rows, wz), f32),
        in_specs=[hbm],
        out_specs=hbm,
        scratch_shapes=[pltpu.VMEM((wx, drives, length), f32), pltpu.VMEM((wx * drives * rows, wz), f32), dma((wx,)), dma((wx,))],
        compiler_params=pltpu.CompilerParams(vmem_limit_bytes=60 * 2**20),
        name="spread",
    )(dense)
    return spread.reshape(populations.shape)


def solution(mesh):
    placed = (
        P("kx", None, None, "ky", "kz"),
        P("kx", None, None, "ky", "kz"),
        P("kx", None, "ky", "kz"),
        P(),
        P("kx", "ky", "kz", None, None),
        P("kx", "ky", "kz", None, None),
        P("kx", "ky", "kz", None, None),
        P("kx", "ky", "kz", None),
    )
    sizes = tuple(mesh.shape[a] for a in ("kx", "ky", "kz"))
    return jax.shard_map(
        functools.partial(per_device, sizes),
        mesh=mesh,
        in_specs=placed,
        out_specs=P("kx", None, None, "ky", "kz"),
        check_vma=False,
    )
```

```python
import functools
import jax
import jax.numpy as jnp
from jax import lax
from jax.experimental import pallas as pl
from jax.experimental.pallas import tpu as pltpu
from jax.sharding import PartitionSpec as P

ITERS = 2
MESH = pl.DeviceIdType.MESH
LANES = 128


def roll(v, by):
    by = by % LANES
    return v if by == 0 else pltpu.roll(v, by, axis=1)


def main_kernel(sizes, pop, force, rate, tiles, send_hbm, target_hbm, tile_hbm, count_hbm, out,
                send_planes, recv_target, recv_tile, recv_count, pop_in, force_in, rate_in, tiles_in, ext, mid, field, base, y_out, y_in, z_out, z_in,
                p_out, p_in, in_sem, pop_sem, tile_sem, x_send, x_recv, y_send, y_recv, z_send, z_recv, p_send, p_recv):
    n_x, n_y, n_z, wx, drives, bands, wy, wz, cap, n_tiles = sizes
    rows = bands * wy
    length = rows * wz
    pieces = length // LANES
    per = LANES // wz
    halves = wy // per
    chunks = p_in.shape[1]
    wide = length // chunks
    mx, my, mz = lax.axis_index("kx"), lax.axis_index("ky"), lax.axis_index("kz")

    def around(me, size, by):
        return lax.rem(me + (by % size), size)

    barrier = pltpu.get_barrier_semaphore()
    friends = []
    for name, me, size, offsets in (("kx", mx, n_x, {1, n_x - 1}), ("ky", my, n_y, {1, n_y - 1}), ("kz", mz, n_z, set(range(1, n_z)))):
        for by in sorted(offsets):
            friends.append({name: around(me, size, by)})
    for friend in friends:
        pl.semaphore_signal(barrier, inc=1, device_id=friend, device_id_type=MESH)

    pop_rows = drives * rows
    pop_loads = [pltpu.make_async_copy(pop.at[pl.ds(x * pop_rows, pop_rows)], pop_in.at[pl.ds(x * pop_rows, pop_rows)], pop_sem.at[x])
                 for x in range(wx)]
    for load in pop_loads:
        load.start()
    pairs = ((send_hbm, send_planes), (target_hbm, recv_target), (tile_hbm, recv_tile), (count_hbm, recv_count), (force, force_in), (rate, rate_in))
    loads = [pltpu.make_async_copy(a, b, in_sem.at[i]) for i, (a, b) in enumerate(pairs)]
    for load in loads:
        load.start()
    tile_loads = [pltpu.make_async_copy(tiles.at[t], tiles_in.at[t], tile_sem.at[t]) for t in range(n_tiles)]
    for load in tile_loads:
        load.start()

    lane = lax.broadcasted_iota(jnp.int32, (8, LANES), 1)
    z_of = lax.rem(lane, wz)

    for x in range(wx):
        pop_loads[x].wait()
        for v in range(pieces):
            piece = jnp.concatenate(
                [pop_in[pl.ds(x * pop_rows + v * per + i, drives, stride=rows), :] for i in range(per)], axis=1)
            ext[0, x + 2, :, v * LANES:(v + 1) * LANES] = piece
            mid[x, :, v * LANES:(v + 1) * LANES] = piece
    loads[0].wait()
    pl.semaphore_wait(barrier, len(friends))

    sel = None
    in_flight = []
    for it in range(ITERS):
        cur = ext.at[it]
        waits_p = [[] for _ in range(chunks)]
        for k in range(n_z - 1, -1, -1):
            peer = around(mz, n_z, k)
            blocks = jnp.concatenate(
                [mid[send_planes[0, 0, 0, c, peer]] for c in range(cap)], axis=0).astype(jnp.bfloat16)
            part = pl.ds(k * cap * drives, cap * drives)
            for q in range(chunks):
                piece = blocks[:, q * wide:(q + 1) * wide]
                if k == 0:
                    p_in[it, q, 0:cap * drives, :] = piece
                else:
                    p_out[it, q, k * cap * drives:(k + 1) * cap * drives, :] = piece
                    waits_p[q].append(pltpu.make_async_remote_copy(
                        p_out.at[it, q, part], p_in.at[it, q, part], p_send.at[it, q, k], p_recv.at[it, q, k],
                        device_id={"kz": peer}, device_id_type=MESH))
        early = (chunks + 1) // 2
        for q in range(early):
            for copy in waits_p[q]:
                copy.start()
        waits_h = [
            pltpu.make_async_remote_copy(
                cur.at[wx:wx + 2], cur.at[0:2], x_send.at[it, 0], x_recv.at[it, 0],
                device_id={"kx": around(mx, n_x, 1)}, device_id_type=MESH),
            pltpu.make_async_remote_copy(
                cur.at[2:4], cur.at[wx + 2:wx + 4], x_send.at[it, 1], x_recv.at[it, 1],
                device_id={"kx": around(mx, n_x, -1)}, device_id_type=MESH)]
        for copy in waits_h:
            copy.start()

        width = 2 * wz
        for x0 in range(0, wx, 2):
            ups, downs = [], []
            for x in (x0, x0 + 1):
                part = [cur[x + 2, :, v * LANES:(v + 1) * LANES] for v in range(pieces)]
                up_z = jnp.zeros((drives, LANES), jnp.float32)
                down_z = up_z
                for v in range(pieces):
                    c = part[v]
                    last = jnp.where(z_of == wz - 2, c - 8.0 * roll(c, -1), c)
                    first = jnp.where(z_of == 0, -c, 8.0 * roll(c, 1) - c)
                    here = lax.div(z_of, 2) == v
                    up_z = jnp.where(here, roll(last, 2 * v - (wz - 2)), up_z)
                    down_z = jnp.where(here, roll(first, 2 * v), down_z)
                ups.append(up_z)
                downs.append(down_z)
                up_y = jnp.zeros((drives, LANES), jnp.float32)
                down_y = up_y
                for b in range(bands):
                    here = lax.div(lane, width) == b
                    up_y = jnp.where(here, roll(part[b * halves + halves - 1], width * b - (LANES - width)), up_y)
                    down_y = jnp.where(here, roll(part[b * halves], width * b), down_y)
                y_out[it, 0, x] = up_y
                y_out[it, 1, x] = down_y
            z_out[it, 0, x0 * drives:(x0 + 2) * drives] = jnp.concatenate(ups, axis=0).astype(jnp.bfloat16)
            z_out[it, 1, x0 * drives:(x0 + 2) * drives] = jnp.concatenate(downs, axis=0).astype(jnp.bfloat16)

        for name, me, size, o, i, ss, rs in (("kz", mz, n_z, z_out, z_in, z_send, z_recv), ("ky", my, n_y, y_out, y_in, y_send, y_recv)):
            for way in range(2):
                copy = pltpu.make_async_remote_copy(
                    o.at[it, way], i.at[it, way], ss.at[it, way], rs.at[it, way],
                    device_id={name: around(me, size, 1 if way == 0 else -1)}, device_id_type=MESH)
                copy.start()
                waits_h.append(copy)
        for q in range(early, chunks):
            for copy in waits_p[q]:
                copy.start()

        if it == 0:
            for load in loads[1:]:
                load.wait()
            for v in range(pieces):
                at = slice(v * LANES, (v + 1) * LANES)
                for a in range(4):
                    source, first, stride = (force_in, a * rows, 3 * rows) if a < 3 else (rate_in, 0, rows)
                    piece = jnp.concatenate(
                        [source[pl.ds(first + v * per + i, wx, stride=stride), :] for i in range(per)], axis=1)
                    if a < 3:
                        piece = piece * (1.0 / 12.0)
                    for x in range(wx):
                        field[a, x, :, at] = jnp.broadcast_to(piece[x:x + 1], (drives, LANES))
            slots = n_z * cap
            col = lax.broadcasted_iota(jnp.int32, (8, slots * drives), 1)
            pair = jnp.full((8, slots * drives), -1, jnp.int32)
            for k in range(n_z):
                source = around(mz, n_z, -k)
                count = recv_count[0, 0, 0, source]
                for c in range(cap):
                    code = jnp.where(c < count, recv_tile[0, 0, 0, c, source] * wx + recv_target[0, 0, 0, c, source], -1)
                    pair = jnp.where(lax.div(col, drives) == k * cap + c, code, pair)
            row = lax.broadcasted_iota(jnp.int32, (n_tiles * wx * drives, slots * drives), 0)
            col = lax.broadcasted_iota(jnp.int32, (n_tiles * wx * drives, slots * drives), 1)
            hit = (lax.div(row, drives) == pair[0:1]) & (lax.rem(row, drives) == lax.rem(col, drives))
            sel = jnp.where(hit, 1.0, 0.0).astype(jnp.bfloat16)

        for copy in waits_h:
            copy.wait_recv()

        def step(pair_at, carry):
            both = pl.ds(pl.multiple_of(pair_at * 2 * drives, 2 * drives), 2 * drives)
            zps, zns = z_in[it, 0, both].astype(jnp.float32), z_in[it, 1, both].astype(jnp.float32)
            for j in range(2):
                x = pair_at * 2 + j
                zp, zn = zps[j * drives:(j + 1) * drives], zns[j * drives:(j + 1) * drives]
                yp, yn = y_in[it, 0, x], y_in[it, 1, x]
                part = [cur[x + 2, :, v * LANES:(v + 1) * LANES] for v in range(pieces)]
                for v in range(pieces):
                    at = slice(v * LANES, (v + 1) * LANES)
                    b, h = divmod(v, halves)
                    c = part[v]
                    dx = 8.0 * (cur[x + 3, :, at] - cur[x + 1, :, at]) - (cur[x + 4, :, at] - cur[x, :, at])
                    after = part[v + 1] if h < halves - 1 else roll(yn, -width * b)
                    before = part[v - 1] if h > 0 else roll(yp, LANES - width - width * b)
                    y1 = roll(jnp.where(lane < wz, after, c), -wz)
                    y2 = roll(jnp.where(lane < 2 * wz, after, c), -2 * wz)
                    w1 = roll(jnp.where(lane >= LANES - wz, before, c), wz)
                    w2 = roll(jnp.where(lane >= LANES - 2 * wz, before, c), 2 * wz)
                    dy = 8.0 * (y1 - w1) - (y2 - w2)
                    a1 = jnp.where(z_of < wz - 1, roll(c, -1), 0.0)
                    b1 = jnp.where(z_of >= 1, roll(c, 1), 0.0)
                    a2 = jnp.where(z_of < wz - 2, roll(c, -2), 0.0)
                    b2 = jnp.where(z_of >= 2, roll(c, 2), 0.0)
                    edge = jnp.where(z_of < 2, roll(zp, -2 * v), jnp.where(z_of >= wz - 2, roll(zn, wz - 2 - 2 * v), 0.0))
                    dz = 8.0 * (a1 - b1) - (a2 - b2) + edge
                    fx, fy, fz, r = (field[a, x, :, at] for a in range(4))
                    base[pl.ds(pl.multiple_of(x * drives, drives), drives), at] = c - (fx * dx + fy * dy + fz * dz) - r * c
            return carry

        lax.fori_loop(0, wx // 2, step, 0)

        m = wx * drives
        total = base[...]
        for q in range(chunks):
            for copy in waits_p[q]:
                copy.wait_recv()
            grouped = jnp.dot(sel, p_in[it, q], preferred_element_type=jnp.float32).astype(jnp.bfloat16)
            for t in range(n_tiles):
                if it == 0 and q == 0:
                    tile_loads[t].wait()
                total = total + lax.dot_general(
                    grouped[t * m:(t + 1) * m], tiles_in[t, :, q * wide:(q + 1) * wide],
                    (((1,), (1,)), ((), ())), preferred_element_type=jnp.float32)
        total = total.reshape(wx, drives, length)
        if it == ITERS - 1:
            out[...] = total
        else:
            ext[it + 1, 2:wx + 2] = total
            mid[...] = total
        in_flight += sum(waits_p, []) + waits_h
    for copy in in_flight:
        copy.wait_send()


def spread_kernel(sizes, dense_hbm, out, dense, laid, in_sem, sem):
    wx, drives, rows, wz = sizes
    per = LANES // wz
    pieces = rows // per
    loads = [pltpu.make_async_copy(dense_hbm.at[x], dense.at[x], in_sem.at[x]) for x in range(wx)]
    for load in loads:
        load.start()
    copies = []
    for x in range(wx):
        loads[x].wait()
        for v in range(pieces):
            piece = dense[x, :, v * LANES:(v + 1) * LANES]
            for i in range(per):
                laid[pl.ds(x * drives * rows + v * per + i, drives, stride=rows), :] = roll(piece, -i * wz)[:, :wz]
        part = pl.ds(x * drives * rows, drives * rows)
        copies.append(pltpu.make_async_copy(laid.at[part], out.at[part], sem.at[x]))
        copies[-1].start()
    for copy in copies:
        copy.wait()


def per_device(mesh_shape, populations, force, rate, tiles, send_planes, recv_target, recv_tile, recv_count):
    wx, drives, bands, wy, wz = populations.shape
    cap = send_planes.shape[-1]
    n_tiles, length, _ = tiles.shape
    n_x, n_y, n_z = mesh_shape
    rows = bands * wy
    sizes = (n_x, n_y, n_z, wx, drives, bands, wy, wz, cap, n_tiles)
    vmem = pl.BlockSpec(memory_space=pltpu.VMEM)
    chunks = bands if n_z <= 8 else 1
    hbm = pl.BlockSpec(memory_space=pltpu.HBM)
    f32, b16 = jnp.float32, jnp.bfloat16
    dma = pltpu.SemaphoreType.DMA
    dense = pl.pallas_call(
        functools.partial(main_kernel, sizes),
        out_shape=jax.ShapeDtypeStruct((wx, drives, length), f32),
        in_specs=[hbm] * 8,
        out_specs=vmem,
        scratch_shapes=[
            pltpu.SMEM((1, 1, 1, cap, n_z), jnp.int32),
            pltpu.SMEM((1, 1, 1, cap, n_z), jnp.int32),
            pltpu.SMEM((1, 1, 1, cap, n_z), jnp.int32),
            pltpu.SMEM((1, 1, 1, n_z), jnp.int32),
            pltpu.VMEM((wx * drives * rows, wz), f32),
            pltpu.VMEM((wx * 3 * rows, wz), f32),
            pltpu.VMEM((wx * rows, wz), f32),
            pltpu.VMEM(tiles.shape, b16),
            pltpu.VMEM((ITERS, wx + 4, drives, length), f32),
            pltpu.VMEM((wx, drives, length), f32),
            pltpu.VMEM((4, wx, drives, length), f32),
            pltpu.VMEM((wx * drives, length), f32),
            pltpu.VMEM((ITERS, 2, wx, drives, LANES), f32),
            pltpu.VMEM((ITERS, 2, wx, drives, LANES), f32),
            pltpu.VMEM((ITERS, 2, wx * drives, LANES), b16),
            pltpu.VMEM((ITERS, 2, wx * drives, LANES), b16),
            pltpu.VMEM((ITERS, chunks, n_z * cap * drives, length // chunks), b16),
            pltpu.VMEM((ITERS, chunks, n_z * cap * drives, length // chunks), b16),
            dma((6,)), dma((wx,)), dma((n_tiles,)),
            dma((ITERS, 2)), dma((ITERS, 2)), dma((ITERS, 2)), dma((ITERS, 2)), dma((ITERS, 2)), dma((ITERS, 2)),
            dma((ITERS, chunks, n_z)), dma((ITERS, chunks, n_z)),
        ],
        compiler_params=pltpu.CompilerParams(collective_id=0, has_side_effects=True, vmem_limit_bytes=60 * 2**20),
        name="steps",
    )(
        populations.reshape(wx * drives * rows, wz),
        force.reshape(wx * 3 * rows, wz),
        rate.reshape(wx * rows, wz),
        tiles,
        jnp.swapaxes(send_planes, -1, -2),
        jnp.swapaxes(recv_target, -1, -2),
        jnp.swapaxes(recv_tile, -1, -2),
        recv_count,
    )
    spread = pl.pallas_call(
        functools.partial(spread_kernel, (wx, drives, rows, wz)),
        out_shape=jax.ShapeDtypeStruct((wx * drives * rows, wz), f32),
        in_specs=[hbm],
        out_specs=hbm,
        scratch_shapes=[pltpu.VMEM((wx, drives, length), f32), pltpu.VMEM((wx * drives * rows, wz), f32), dma((wx,)), dma((wx,))],
        compiler_params=pltpu.CompilerParams(vmem_limit_bytes=60 * 2**20),
        name="spread",
    )(dense)
    return spread.reshape(populations.shape)


def solution(mesh):
    placed = (
        P("kx", None, None, "ky", "kz"),
        P("kx", None, None, "ky", "kz"),
        P("kx", None, "ky", "kz"),
        P(),
        P("kx", "ky", "kz", None, None),
        P("kx", "ky", "kz", None, None),
        P("kx", "ky", "kz", None, None),
        P("kx", "ky", "kz", None),
    )
    sizes = tuple(mesh.shape[a] for a in ("kx", "ky", "kz"))
    return jax.shard_map(
        functools.partial(per_device, sizes),
        mesh=mesh,
        in_specs=placed,
        out_specs=P("kx", None, None, "ky", "kz"),
        check_vma=False,
    )
```

```python
import functools
import jax
import jax.numpy as jnp
from jax import lax
from jax.experimental import pallas as pl
from jax.experimental.pallas import tpu as pltpu
from jax.sharding import PartitionSpec as P

ITERS = 2
MESH = pl.DeviceIdType.MESH
LANES = 128


def roll(v, by):
    by = by % LANES
    return v if by == 0 else pltpu.roll(v, by, axis=1)


def main_kernel(sizes, pop, force, rate, tiles, send_hbm, target_hbm, tile_hbm, count_hbm, out,
                send_planes, recv_target, recv_tile, recv_count, pop_in, force_in, rate_in, tiles_in, ext, mid, field, sel, base, y_out, y_in, z_out, z_in,
                p_out, p_in, in_sem, pop_sem, tile_sem, x_send, x_recv, y_send, y_recv, z_send, z_recv, p_send, p_recv):
    n_x, n_y, n_z, wx, drives, bands, wy, wz, cap, n_tiles = sizes
    rows = bands * wy
    length = rows * wz
    pieces = length // LANES
    per = LANES // wz
    halves = wy // per
    chunks = p_in.shape[1]
    wide = length // chunks
    mx, my, mz = lax.axis_index("kx"), lax.axis_index("ky"), lax.axis_index("kz")

    def around(me, size, by):
        return lax.rem(me + (by % size), size)

    barrier = pltpu.get_barrier_semaphore()
    friends = []
    for name, me, size, offsets in (("kx", mx, n_x, {1, n_x - 1}), ("ky", my, n_y, {1, n_y - 1}), ("kz", mz, n_z, set(range(1, n_z)))):
        for by in sorted(offsets):
            friends.append({name: around(me, size, by)})
    for friend in friends:
        pl.semaphore_signal(barrier, inc=1, device_id=friend, device_id_type=MESH)

    pop_rows = drives * rows

    def pop_load(x):
        part = pl.ds(pl.multiple_of(x * pop_rows, 8), pop_rows)
        return pltpu.make_async_copy(pop.at[part], pop_in.at[part], pop_sem.at[x])

    for x in range(wx):
        pop_load(x).start()
    pairs = ((send_hbm, send_planes), (target_hbm, recv_target), (tile_hbm, recv_tile), (count_hbm, recv_count), (force, force_in), (rate, rate_in))
    loads = [pltpu.make_async_copy(a, b, in_sem.at[i]) for i, (a, b) in enumerate(pairs)]
    for load in loads:
        load.start()
    tile_loads = [pltpu.make_async_copy(tiles.at[t], tiles_in.at[t], tile_sem.at[t]) for t in range(n_tiles)]
    for load in tile_loads:
        load.start()

    lane = lax.broadcasted_iota(jnp.int32, (8, LANES), 1)
    z_of = lax.rem(lane, wz)

    def lay_pop(x, carry):
        pop_load(x).wait()
        for v in range(pieces):
            piece = jnp.concatenate(
                [pop_in[pl.ds(x * pop_rows + v * per + i, drives, stride=rows), :] for i in range(per)], axis=1)
            ext[0, x + 2, :, v * LANES:(v + 1) * LANES] = piece
            mid[x, :, v * LANES:(v + 1) * LANES] = piece
        return carry

    lax.fori_loop(0, wx, lay_pop, 0)
    loads[0].wait()
    pl.semaphore_wait(barrier, len(friends))

    early = (chunks + 1) // 2
    width = 2 * wz
    m = wx * drives

    def plane_copies(it, q):
        copies = []
        for k in range(n_z - 1, 0, -1):
            part = pl.ds(k * cap * drives, cap * drives)
            copies.append(pltpu.make_async_remote_copy(
                p_out.at[it, q, part], p_in.at[it, q, part], p_send.at[it, q, k], p_recv.at[it, q, k],
                device_id={"kz": around(mz, n_z, k)}, device_id_type=MESH))
        return copies

    def x_copies(it):
        cur = ext.at[it]
        return [
            pltpu.make_async_remote_copy(
                cur.at[wx:wx + 2], cur.at[0:2], x_send.at[it, 0], x_recv.at[it, 0],
                device_id={"kx": around(mx, n_x, 1)}, device_id_type=MESH),
            pltpu.make_async_remote_copy(
                cur.at[2:4], cur.at[wx + 2:wx + 4], x_send.at[it, 1], x_recv.at[it, 1],
                device_id={"kx": around(mx, n_x, -1)}, device_id_type=MESH)]

    def edge_copies(it):
        copies = []
        for name, me, size, o, i, ss, rs in (("kz", mz, n_z, z_out, z_in, z_send, z_recv), ("ky", my, n_y, y_out, y_in, y_send, y_recv)):
            for way in range(2):
                copies.append(pltpu.make_async_remote_copy(
                    o.at[it, way], i.at[it, way], ss.at[it, way], rs.at[it, way],
                    device_id={name: around(me, size, 1 if way == 0 else -1)}, device_id_type=MESH))
        return copies

    def time_step(it, carry):
        cur = ext.at[it]
        for copy in x_copies(it):
            copy.start()
        for k in range(n_z - 1, -1, -1):
            peer = around(mz, n_z, k)
            blocks = jnp.concatenate(
                [mid[send_planes[0, 0, 0, c, peer]] for c in range(cap)], axis=0).astype(jnp.bfloat16)
            to = p_in if k == 0 else p_out
            for q in range(chunks):
                to[it, q, k * cap * drives:(k + 1) * cap * drives, :] = blocks[:, q * wide:(q + 1) * wide]
        for q in range(early):
            for copy in plane_copies(it, q):
                copy.start()

        def pack(pair_at, carry):
            both = pl.ds(pl.multiple_of(pair_at * 2 * drives, 2 * drives), 2 * drives)
            ups, downs = [], []
            for j in range(2):
                x = pair_at * 2 + j
                part = [cur[x + 2, :, v * LANES:(v + 1) * LANES] for v in range(pieces)]
                up_z = jnp.zeros((drives, LANES), jnp.float32)
                down_z = up_z
                for v in range(pieces):
                    c = part[v]
                    last = jnp.where(z_of == wz - 2, c - 8.0 * roll(c, -1), c)
                    first = jnp.where(z_of == 0, -c, 8.0 * roll(c, 1) - c)
                    here = lax.div(z_of, 2) == v
                    up_z = jnp.where(here, roll(last, 2 * v - (wz - 2)), up_z)
                    down_z = jnp.where(here, roll(first, 2 * v), down_z)
                ups.append(up_z)
                downs.append(down_z)
                up_y = jnp.zeros((drives, LANES), jnp.float32)
                down_y = up_y
                for b in range(bands):
                    here = lax.div(lane, width) == b
                    up_y = jnp.where(here, roll(part[b * halves + halves - 1], width * b - (LANES - width)), up_y)
                    down_y = jnp.where(here, roll(part[b * halves], width * b), down_y)
                y_out[it, 0, x] = up_y
                y_out[it, 1, x] = down_y
            z_out[it, 0, both] = jnp.concatenate(ups, axis=0).astype(jnp.bfloat16)
            z_out[it, 1, both] = jnp.concatenate(downs, axis=0).astype(jnp.bfloat16)
            return carry

        lax.fori_loop(0, wx // 2, pack, 0)
        for copy in edge_copies(it):
            copy.start()
        for q in range(early, chunks):
            for copy in plane_copies(it, q):
                copy.start()

        @pl.when(it == 0)
        def _():
            for load in loads[1:]:
                load.wait()

            def lay_field(v, carry):
                at = pl.ds(pl.multiple_of(v * LANES, LANES), LANES)
                for a in range(4):
                    source, first, stride = (force_in, a * rows, 3 * rows) if a < 3 else (rate_in, 0, rows)
                    piece = jnp.concatenate(
                        [source[pl.ds(first + v * per + i, wx, stride=stride), :] for i in range(per)], axis=1)
                    if a < 3:
                        piece = piece * (1.0 / 12.0)
                    for x in range(wx):
                        field[a, x, :, at] = jnp.broadcast_to(piece[x:x + 1], (drives, LANES))
                return carry

            lax.fori_loop(0, pieces, lay_field, 0)
            slots = n_z * cap
            col = lax.broadcasted_iota(jnp.int32, (8, slots * drives), 1)
            pair = jnp.full((8, slots * drives), -1, jnp.int32)
            for k in range(n_z):
                source = around(mz, n_z, -k)
                count = recv_count[0, 0, 0, source]
                for c in range(cap):
                    code = jnp.where(c < count, recv_tile[0, 0, 0, c, source] * wx + recv_target[0, 0, 0, c, source], -1)
                    pair = jnp.where(lax.div(col, drives) == k * cap + c, code, pair)
            row = lax.broadcasted_iota(jnp.int32, (n_tiles * m, slots * drives), 0)
            col = lax.broadcasted_iota(jnp.int32, (n_tiles * m, slots * drives), 1)
            hit = (lax.div(row, drives) == pair[0:1]) & (lax.rem(row, drives) == lax.rem(col, drives))
            sel[...] = jnp.where(hit, 1.0, 0.0).astype(jnp.bfloat16)

        for copy in x_copies(it) + edge_copies(it):
            copy.wait_recv()

        def step(pair_at, carry):
            both = pl.ds(pl.multiple_of(pair_at * 2 * drives, 2 * drives), 2 * drives)
            zps, zns = z_in[it, 0, both].astype(jnp.float32), z_in[it, 1, both].astype(jnp.float32)
            for j in range(2):
                x = pair_at * 2 + j
                zp, zn = zps[j * drives:(j + 1) * drives], zns[j * drives:(j + 1) * drives]
                yp, yn = y_in[it, 0, x], y_in[it, 1, x]
                part = [cur[x + 2, :, v * LANES:(v + 1) * LANES] for v in range(pieces)]
                for v in range(pieces):
                    at = slice(v * LANES, (v + 1) * LANES)
                    b, h = divmod(v, halves)
                    c = part[v]
                    dx = 8.0 * (cur[x + 3, :, at] - cur[x + 1, :, at]) - (cur[x + 4, :, at] - cur[x, :, at])
                    after = part[v + 1] if h < halves - 1 else roll(yn, -width * b)
                    before = part[v - 1] if h > 0 else roll(yp, LANES - width - width * b)
                    y1 = roll(jnp.where(lane < wz, after, c), -wz)
                    y2 = roll(jnp.where(lane < 2 * wz, after, c), -2 * wz)
                    w1 = roll(jnp.where(lane >= LANES - wz, before, c), wz)
                    w2 = roll(jnp.where(lane >= LANES - 2 * wz, before, c), 2 * wz)
                    dy = 8.0 * (y1 - w1) - (y2 - w2)
                    a1 = jnp.where(z_of < wz - 1, roll(c, -1), 0.0)
                    b1 = jnp.where(z_of >= 1, roll(c, 1), 0.0)
                    a2 = jnp.where(z_of < wz - 2, roll(c, -2), 0.0)
                    b2 = jnp.where(z_of >= 2, roll(c, 2), 0.0)
                    edge = jnp.where(z_of < 2, roll(zp, -2 * v), jnp.where(z_of >= wz - 2, roll(zn, wz - 2 - 2 * v), 0.0))
                    dz = 8.0 * (a1 - b1) - (a2 - b2) + edge
                    fx, fy, fz, r = (field[a, x, :, at] for a in range(4))
                    base[pl.ds(pl.multiple_of(x * drives, drives), drives), at] = c - (fx * dx + fy * dy + fz * dz) - r * c
            return carry

        lax.fori_loop(0, wx // 2, step, 0)

        @pl.when(it == 0)
        def _():
            for load in tile_loads:
                load.wait()

        def product(q, carry):
            for copy in plane_copies(it, q):
                copy.wait_recv()
            at = pl.ds(pl.multiple_of(q * wide, LANES), wide)
            grouped = jnp.dot(sel[...], p_in[it, q], preferred_element_type=jnp.float32).astype(jnp.bfloat16)
            total = base[...]
            for t in range(n_tiles):
                total = total + lax.dot_general(
                    grouped[t * m:(t + 1) * m], tiles_in[t, :, at],
                    (((1,), (1,)), ((), ())), preferred_element_type=jnp.float32)
            base[...] = total
            return carry

        lax.fori_loop(0, chunks, product, 0)
        total = base[...].reshape(wx, drives, length)
        ext[it + 1, 2:wx + 2] = total
        mid[...] = total
        return carry

    lax.fori_loop(0, ITERS, time_step, 0)
    result = pltpu.make_async_copy(mid, out, in_sem.at[0])
    result.start()

    def drain(it, carry):
        for copy in x_copies(it) + edge_copies(it):
            copy.wait_send()
        for q in range(chunks):
            for copy in plane_copies(it, q):
                copy.wait_send()
        return carry

    lax.fori_loop(0, ITERS, drain, 0)
    result.wait()


def spread_kernel(sizes, dense_hbm, out, dense, laid, in_sem, sem):
    wx, drives, rows, wz = sizes
    per = LANES // wz
    pieces = rows // per

    def load(x):
        return pltpu.make_async_copy(dense_hbm.at[x], dense.at[x], in_sem.at[x])

    def store(x):
        part = pl.ds(pl.multiple_of(x * drives * rows, 8), drives * rows)
        return pltpu.make_async_copy(laid.at[part], out.at[part], sem.at[x])

    for x in range(wx):
        load(x).start()

    def lay(x, carry):
        load(x).wait()
        for v in range(pieces):
            piece = dense[x, :, v * LANES:(v + 1) * LANES]
            for i in range(per):
                laid[pl.ds(x * drives * rows + v * per + i, drives, stride=rows), :] = roll(piece, -i * wz)[:, :wz]
        store(x).start()
        return carry

    lax.fori_loop(0, wx, lay, 0)
    for x in range(wx):
        store(x).wait()


def per_device(mesh_shape, populations, force, rate, tiles, send_planes, recv_target, recv_tile, recv_count):
    wx, drives, bands, wy, wz = populations.shape
    cap = send_planes.shape[-1]
    n_tiles, length, _ = tiles.shape
    n_x, n_y, n_z = mesh_shape
    rows = bands * wy
    sizes = (n_x, n_y, n_z, wx, drives, bands, wy, wz, cap, n_tiles)
    chunks = bands if n_z <= 8 else 1
    hbm = pl.BlockSpec(memory_space=pltpu.HBM)
    f32, b16 = jnp.float32, jnp.bfloat16
    dma = pltpu.SemaphoreType.DMA
    dense = pl.pallas_call(
        functools.partial(main_kernel, sizes),
        out_shape=jax.ShapeDtypeStruct((wx, drives, length), f32),
        in_specs=[hbm] * 8,
        out_specs=hbm,
        scratch_shapes=[
            pltpu.SMEM((1, 1, 1, cap, n_z), jnp.int32),
            pltpu.SMEM((1, 1, 1, cap, n_z), jnp.int32),
            pltpu.SMEM((1, 1, 1, cap, n_z), jnp.int32),
            pltpu.SMEM((1, 1, 1, n_z), jnp.int32),
            pltpu.VMEM((wx * drives * rows, wz), f32),
            pltpu.VMEM((wx * 3 * rows, wz), f32),
            pltpu.VMEM((wx * rows, wz), f32),
            pltpu.VMEM(tiles.shape, b16),
            pltpu.VMEM((ITERS + 1, wx + 4, drives, length), f32),
            pltpu.VMEM((wx, drives, length), f32),
            pltpu.VMEM((4, wx, drives, length), f32),
            pltpu.VMEM((n_tiles * wx * drives, n_z * cap * drives), b16),
            pltpu.VMEM((wx * drives, length), f32),
            pltpu.VMEM((ITERS, 2, wx, drives, LANES), f32),
            pltpu.VMEM((ITERS, 2, wx, drives, LANES), f32),
            pltpu.VMEM((ITERS, 2, wx * drives, LANES), b16),
            pltpu.VMEM((ITERS, 2, wx * drives, LANES), b16),
            pltpu.VMEM((ITERS, chunks, n_z * cap * drives, length // chunks), b16),
            pltpu.VMEM((ITERS, chunks, n_z * cap * drives, length // chunks), b16),
            dma((6,)), dma((wx,)), dma((n_tiles,)),
            dma((ITERS, 2)), dma((ITERS, 2)), dma((ITERS, 2)), dma((ITERS, 2)), dma((ITERS, 2)), dma((ITERS, 2)),
            dma((ITERS, chunks, n_z)), dma((ITERS, chunks, n_z)),
        ],
        compiler_params=pltpu.CompilerParams(collective_id=0, has_side_effects=True, vmem_limit_bytes=60 * 2**20),
        name="steps",
    )(
        populations.reshape(wx * drives * rows, wz),
        force.reshape(wx * 3 * rows, wz),
        rate.reshape(wx * rows, wz),
        tiles,
        jnp.swapaxes(send_planes, -1, -2),
        jnp.swapaxes(recv_target, -1, -2),
        jnp.swapaxes(recv_tile, -1, -2),
        recv_count,
    )
    spread = pl.pallas_call(
        functools.partial(spread_kernel, (wx, drives, rows, wz)),
        out_shape=jax.ShapeDtypeStruct((wx * drives * rows, wz), f32),
        in_specs=[hbm],
        out_specs=hbm,
        scratch_shapes=[pltpu.VMEM((wx, drives, length), f32), pltpu.VMEM((wx * drives * rows, wz), f32), dma((wx,)), dma((wx,))],
        compiler_params=pltpu.CompilerParams(vmem_limit_bytes=60 * 2**20),
        name="spread",
    )(dense)
    return spread.reshape(populations.shape)


def solution(mesh):
    placed = (
        P("kx", None, None, "ky", "kz"),
        P("kx", None, None, "ky", "kz"),
        P("kx", None, "ky", "kz"),
        P(),
        P("kx", "ky", "kz", None, None),
        P("kx", "ky", "kz", None, None),
        P("kx", "ky", "kz", None, None),
        P("kx", "ky", "kz", None),
    )
    sizes = tuple(mesh.shape[a] for a in ("kx", "ky", "kz"))
    return jax.shard_map(
        functools.partial(per_device, sizes),
        mesh=mesh,
        in_specs=placed,
        out_specs=P("kx", None, None, "ky", "kz"),
        check_vma=False,
    )
```

```python
import functools
import jax
import jax.numpy as jnp
from jax import lax
from jax.experimental import pallas as pl
from jax.experimental.pallas import tpu as pltpu
from jax.sharding import PartitionSpec as P

ITERS = 2
MESH = pl.DeviceIdType.MESH
LANES = 128


def roll(v, by):
    by = by % LANES
    return v if by == 0 else pltpu.roll(v, by, axis=1)


def main_kernel(sizes, pop, force, rate, tiles, send_hbm, target_hbm, tile_hbm, count_hbm, out,
                send_planes, recv_target, recv_tile, recv_count, pop_in, force_in, rate_in, tiles_in, ext, mid, field, sel, turned, base, y_out, y_in, z_out, z_in,
                p_out, p_in, in_sem, pop_sem, tile_sem, x_send, x_recv, y_send, y_recv, z_send, z_recv, p_send, p_recv):
    n_x, n_y, n_z, wx, drives, bands, wy, wz, cap, n_tiles = sizes
    rows = bands * wy
    length = rows * wz
    pieces = length // LANES
    per = LANES // wz
    halves = wy // per
    chunks = p_in.shape[1]
    wide = length // chunks
    mx, my, mz = lax.axis_index("kx"), lax.axis_index("ky"), lax.axis_index("kz")

    def around(me, size, by):
        return lax.rem(me + (by % size), size)

    barrier = pltpu.get_barrier_semaphore()
    friends = []
    for name, me, size, offsets in (("kx", mx, n_x, {1, n_x - 1}), ("ky", my, n_y, {1, n_y - 1}), ("kz", mz, n_z, set(range(1, n_z)))):
        for by in sorted(offsets):
            friends.append({name: around(me, size, by)})
    for friend in friends:
        pl.semaphore_signal(barrier, inc=1, device_id=friend, device_id_type=MESH)

    pop_rows = drives * rows

    def pop_load(x):
        part = pl.ds(pl.multiple_of(x * pop_rows, 8), pop_rows)
        return pltpu.make_async_copy(pop.at[part], pop_in.at[part], pop_sem.at[x])

    for x in range(wx):
        pop_load(x).start()
    pairs = ((send_hbm, send_planes), (target_hbm, recv_target), (tile_hbm, recv_tile), (count_hbm, recv_count), (force, force_in), (rate, rate_in))
    loads = [pltpu.make_async_copy(a, b, in_sem.at[i]) for i, (a, b) in enumerate(pairs)]
    for load in loads:
        load.start()
    tile_loads = [pltpu.make_async_copy(tiles.at[t], tiles_in.at[t], tile_sem.at[t]) for t in range(n_tiles)]
    for load in tile_loads:
        load.start()

    lane = lax.broadcasted_iota(jnp.int32, (8, LANES), 1)
    z_of = lax.rem(lane, wz)

    def lay_pop(x, carry):
        pop_load(x).wait()
        for v in range(pieces):
            piece = jnp.concatenate(
                [pop_in[pl.ds(x * pop_rows + v * per + i, drives, stride=rows), :] for i in range(per)], axis=1)
            ext[0, x + 2, :, v * LANES:(v + 1) * LANES] = piece
            mid[x, :, v * LANES:(v + 1) * LANES] = piece
        return carry

    lax.fori_loop(0, wx, lay_pop, 0)
    loads[0].wait()
    pl.semaphore_wait(barrier, len(friends))

    early = (chunks + 1) // 2
    width = 2 * wz
    m = wx * drives

    def plane_copies(it, q):
        copies = []
        for k in range(n_z - 1, 0, -1):
            part = pl.ds(k * cap * drives, cap * drives)
            copies.append(pltpu.make_async_remote_copy(
                p_out.at[it, q, part], p_in.at[it, q, part], p_send.at[it, q, k], p_recv.at[it, q, k],
                device_id={"kz": around(mz, n_z, k)}, device_id_type=MESH))
        return copies

    def x_copies(it):
        cur = ext.at[it]
        return [
            pltpu.make_async_remote_copy(
                cur.at[wx:wx + 2], cur.at[0:2], x_send.at[it, 0], x_recv.at[it, 0],
                device_id={"kx": around(mx, n_x, 1)}, device_id_type=MESH),
            pltpu.make_async_remote_copy(
                cur.at[2:4], cur.at[wx + 2:wx + 4], x_send.at[it, 1], x_recv.at[it, 1],
                device_id={"kx": around(mx, n_x, -1)}, device_id_type=MESH)]

    def edge_copies(it):
        copies = []
        for name, me, size, o, i, ss, rs in (("kz", mz, n_z, z_out, z_in, z_send, z_recv), ("ky", my, n_y, y_out, y_in, y_send, y_recv)):
            for way in range(2):
                copies.append(pltpu.make_async_remote_copy(
                    o.at[it, way], i.at[it, way], ss.at[it, way], rs.at[it, way],
                    device_id={name: around(me, size, 1 if way == 0 else -1)}, device_id_type=MESH))
        return copies

    def time_step(it, carry):
        cur = ext.at[it]
        for copy in x_copies(it):
            copy.start()
        for k in range(n_z - 1, -1, -1):
            peer = around(mz, n_z, k)
            blocks = jnp.concatenate(
                [mid[send_planes[0, 0, 0, c, peer]] for c in range(cap)], axis=0).astype(jnp.bfloat16)
            to = p_in if k == 0 else p_out
            for q in range(chunks):
                to[it, q, k * cap * drives:(k + 1) * cap * drives, :] = blocks[:, q * wide:(q + 1) * wide]
        for q in range(early):
            for copy in plane_copies(it, q):
                copy.start()

        def pack(pair_at, carry):
            both = pl.ds(pl.multiple_of(pair_at * 2 * drives, 2 * drives), 2 * drives)
            ups, downs = [], []
            for j in range(2):
                x = pair_at * 2 + j
                part = [cur[x + 2, :, v * LANES:(v + 1) * LANES] for v in range(pieces)]
                up_z = jnp.zeros((drives, LANES), jnp.float32)
                down_z = up_z
                for v in range(pieces):
                    c = part[v]
                    last = jnp.where(z_of == wz - 2, c - 8.0 * roll(c, -1), c)
                    first = jnp.where(z_of == 0, -c, 8.0 * roll(c, 1) - c)
                    here = lax.div(z_of, 2) == v
                    up_z = jnp.where(here, roll(last, 2 * v - (wz - 2)), up_z)
                    down_z = jnp.where(here, roll(first, 2 * v), down_z)
                ups.append(up_z)
                downs.append(down_z)
                up_y = jnp.zeros((drives, LANES), jnp.float32)
                down_y = up_y
                for b in range(bands):
                    here = lax.div(lane, width) == b
                    up_y = jnp.where(here, roll(part[b * halves + halves - 1], width * b - (LANES - width)), up_y)
                    down_y = jnp.where(here, roll(part[b * halves], width * b), down_y)
                y_out[it, 0, x] = up_y
                y_out[it, 1, x] = down_y
            z_out[it, 0, both] = jnp.concatenate(ups, axis=0).astype(jnp.bfloat16)
            z_out[it, 1, both] = jnp.concatenate(downs, axis=0).astype(jnp.bfloat16)
            return carry

        lax.fori_loop(0, wx // 2, pack, 0)
        for copy in edge_copies(it):
            copy.start()
        for q in range(early, chunks):
            for copy in plane_copies(it, q):
                copy.start()

        @pl.when(it == 0)
        def _():
            for load in loads[1:]:
                load.wait()

            def lay_field(v, carry):
                at = pl.ds(pl.multiple_of(v * LANES, LANES), LANES)
                for a in range(4):
                    source, first, stride = (force_in, a * rows, 3 * rows) if a < 3 else (rate_in, 0, rows)
                    piece = jnp.concatenate(
                        [source[pl.ds(first + v * per + i, wx, stride=stride), :] for i in range(per)], axis=1)
                    if a < 3:
                        piece = piece * (1.0 / 12.0)
                    for x in range(wx):
                        field[a, x, :, at] = jnp.broadcast_to(piece[x:x + 1], (drives, LANES))
                return carry

            lax.fori_loop(0, pieces, lay_field, 0)
            slots = n_z * cap
            col = lax.broadcasted_iota(jnp.int32, (8, slots * drives), 1)
            pair = jnp.full((8, slots * drives), -1, jnp.int32)
            for k in range(n_z):
                source = around(mz, n_z, -k)
                count = recv_count[0, 0, 0, source]
                for c in range(cap):
                    code = jnp.where(c < count, recv_tile[0, 0, 0, c, source] * wx + recv_target[0, 0, 0, c, source], -1)
                    pair = jnp.where(lax.div(col, drives) == k * cap + c, code, pair)
            row = lax.broadcasted_iota(jnp.int32, (n_tiles * m, slots * drives), 0)
            col = lax.broadcasted_iota(jnp.int32, (n_tiles * m, slots * drives), 1)
            hit = (lax.div(row, drives) == pair[0:1]) & (lax.rem(row, drives) == lax.rem(col, drives))
            sel[...] = jnp.where(hit, 1.0, 0.0).astype(jnp.bfloat16)

        for copy in x_copies(it) + edge_copies(it):
            copy.wait_recv()

        def step(pair_at, carry):
            both = pl.ds(pl.multiple_of(pair_at * 2 * drives, 2 * drives), 2 * drives)
            zps, zns = z_in[it, 0, both].astype(jnp.float32), z_in[it, 1, both].astype(jnp.float32)
            for j in range(2):
                x = pair_at * 2 + j
                zp, zn = zps[j * drives:(j + 1) * drives], zns[j * drives:(j + 1) * drives]
                yp, yn = y_in[it, 0, x], y_in[it, 1, x]
                part = [cur[x + 2, :, v * LANES:(v + 1) * LANES] for v in range(pieces)]
                for v in range(pieces):
                    at = slice(v * LANES, (v + 1) * LANES)
                    b, h = divmod(v, halves)
                    c = part[v]
                    dx = 8.0 * (cur[x + 3, :, at] - cur[x + 1, :, at]) - (cur[x + 4, :, at] - cur[x, :, at])
                    after = part[v + 1] if h < halves - 1 else roll(yn, -width * b)
                    before = part[v - 1] if h > 0 else roll(yp, LANES - width - width * b)
                    y1 = roll(jnp.where(lane < wz, after, c), -wz)
                    y2 = roll(jnp.where(lane < 2 * wz, after, c), -2 * wz)
                    w1 = roll(jnp.where(lane >= LANES - wz, before, c), wz)
                    w2 = roll(jnp.where(lane >= LANES - 2 * wz, before, c), 2 * wz)
                    dy = 8.0 * (y1 - w1) - (y2 - w2)
                    a1 = jnp.where(z_of < wz - 1, roll(c, -1), 0.0)
                    b1 = jnp.where(z_of >= 1, roll(c, 1), 0.0)
                    a2 = jnp.where(z_of < wz - 2, roll(c, -2), 0.0)
                    b2 = jnp.where(z_of >= 2, roll(c, 2), 0.0)
                    edge = jnp.where(z_of < 2, roll(zp, -2 * v), jnp.where(z_of >= wz - 2, roll(zn, wz - 2 - 2 * v), 0.0))
                    dz = 8.0 * (a1 - b1) - (a2 - b2) + edge
                    fx, fy, fz, r = (field[a, x, :, at] for a in range(4))
                    base[pl.ds(pl.multiple_of(x * drives, drives), drives), at] = c - (fx * dx + fy * dy + fz * dz) - r * c
            return carry

        lax.fori_loop(0, wx // 2, step, 0)

        @pl.when(it == 0)
        def _():
            for load in tile_loads:
                load.wait()

        def product(q, carry):
            for copy in plane_copies(it, q):
                copy.wait_recv()
            at = pl.ds(pl.multiple_of(q * wide, LANES), wide)
            grouped = jnp.dot(sel[...], p_in[it, q], preferred_element_type=jnp.float32).astype(jnp.bfloat16)
            total = None
            for t in range(n_tiles):
                term = lax.dot_general(
                    tiles_in[t, :, at], grouped[t * m:(t + 1) * m],
                    (((1,), (1,)), ((), ())), preferred_element_type=jnp.float32)
                total = term if total is None else total + term
            turned[...] += total
            return carry

        turned[...] = jnp.zeros_like(turned)
        lax.fori_loop(0, chunks, product, 0)
        base[...] += jnp.transpose(turned[...])
        total = base[...].reshape(wx, drives, length)
        ext[it + 1, 2:wx + 2] = total
        mid[...] = total
        return carry

    lax.fori_loop(0, ITERS, time_step, 0)
    result = pltpu.make_async_copy(mid, out, in_sem.at[0])
    result.start()

    def drain(it, carry):
        for copy in x_copies(it) + edge_copies(it):
            copy.wait_send()
        for q in range(chunks):
            for copy in plane_copies(it, q):
                copy.wait_send()
        return carry

    lax.fori_loop(0, ITERS, drain, 0)
    result.wait()


def spread_kernel(sizes, dense_hbm, out, dense, laid, in_sem, sem):
    wx, drives, rows, wz = sizes
    per = LANES // wz
    pieces = rows // per

    def load(x):
        return pltpu.make_async_copy(dense_hbm.at[x], dense.at[x], in_sem.at[x])

    def store(x):
        part = pl.ds(pl.multiple_of(x * drives * rows, 8), drives * rows)
        return pltpu.make_async_copy(laid.at[part], out.at[part], sem.at[x])

    for x in range(wx):
        load(x).start()

    def lay(x, carry):
        load(x).wait()
        for v in range(pieces):
            piece = dense[x, :, v * LANES:(v + 1) * LANES]
            for i in range(per):
                laid[pl.ds(x * drives * rows + v * per + i, drives, stride=rows), :] = roll(piece, -i * wz)[:, :wz]
        store(x).start()
        return carry

    lax.fori_loop(0, wx, lay, 0)
    for x in range(wx):
        store(x).wait()


def per_device(mesh_shape, populations, force, rate, tiles, send_planes, recv_target, recv_tile, recv_count):
    wx, drives, bands, wy, wz = populations.shape
    cap = send_planes.shape[-1]
    n_tiles, length, _ = tiles.shape
    n_x, n_y, n_z = mesh_shape
    rows = bands * wy
    sizes = (n_x, n_y, n_z, wx, drives, bands, wy, wz, cap, n_tiles)
    chunks = bands if n_z <= 8 else 1
    hbm = pl.BlockSpec(memory_space=pltpu.HBM)
    f32, b16 = jnp.float32, jnp.bfloat16
    dma = pltpu.SemaphoreType.DMA
    dense = pl.pallas_call(
        functools.partial(main_kernel, sizes),
        out_shape=jax.ShapeDtypeStruct((wx, drives, length), f32),
        in_specs=[hbm] * 8,
        out_specs=hbm,
        scratch_shapes=[
            pltpu.SMEM((1, 1, 1, cap, n_z), jnp.int32),
            pltpu.SMEM((1, 1, 1, cap, n_z), jnp.int32),
            pltpu.SMEM((1, 1, 1, cap, n_z), jnp.int32),
            pltpu.SMEM((1, 1, 1, n_z), jnp.int32),
            pltpu.VMEM((wx * drives * rows, wz), f32),
            pltpu.VMEM((wx * 3 * rows, wz), f32),
            pltpu.VMEM((wx * rows, wz), f32),
            pltpu.VMEM(tiles.shape, b16),
            pltpu.VMEM((ITERS + 1, wx + 4, drives, length), f32),
            pltpu.VMEM((wx, drives, length), f32),
            pltpu.VMEM((4, wx, drives, length), f32),
            pltpu.VMEM((n_tiles * wx * drives, n_z * cap * drives), b16),
            pltpu.VMEM((length, wx * drives), f32),
            pltpu.VMEM((wx * drives, length), f32),
            pltpu.VMEM((ITERS, 2, wx, drives, LANES), f32),
            pltpu.VMEM((ITERS, 2, wx, drives, LANES), f32),
            pltpu.VMEM((ITERS, 2, wx * drives, LANES), b16),
            pltpu.VMEM((ITERS, 2, wx * drives, LANES), b16),
            pltpu.VMEM((ITERS, chunks, n_z * cap * drives, length // chunks), b16),
            pltpu.VMEM((ITERS, chunks, n_z * cap * drives, length // chunks), b16),
            dma((6,)), dma((wx,)), dma((n_tiles,)),
            dma((ITERS, 2)), dma((ITERS, 2)), dma((ITERS, 2)), dma((ITERS, 2)), dma((ITERS, 2)), dma((ITERS, 2)),
            dma((ITERS, chunks, n_z)), dma((ITERS, chunks, n_z)),
        ],
        compiler_params=pltpu.CompilerParams(collective_id=0, has_side_effects=True, vmem_limit_bytes=60 * 2**20),
        name="steps",
    )(
        populations.reshape(wx * drives * rows, wz),
        force.reshape(wx * 3 * rows, wz),
        rate.reshape(wx * rows, wz),
        tiles,
        jnp.swapaxes(send_planes, -1, -2),
        jnp.swapaxes(recv_target, -1, -2),
        jnp.swapaxes(recv_tile, -1, -2),
        recv_count,
    )
    spread = pl.pallas_call(
        functools.partial(spread_kernel, (wx, drives, rows, wz)),
        out_shape=jax.ShapeDtypeStruct((wx * drives * rows, wz), f32),
        in_specs=[hbm],
        out_specs=hbm,
        scratch_shapes=[pltpu.VMEM((wx, drives, length), f32), pltpu.VMEM((wx * drives * rows, wz), f32), dma((wx,)), dma((wx,))],
        compiler_params=pltpu.CompilerParams(vmem_limit_bytes=60 * 2**20),
        name="spread",
    )(dense)
    return spread.reshape(populations.shape)


def solution(mesh):
    placed = (
        P("kx", None, None, "ky", "kz"),
        P("kx", None, None, "ky", "kz"),
        P("kx", None, "ky", "kz"),
        P(),
        P("kx", "ky", "kz", None, None),
        P("kx", "ky", "kz", None, None),
        P("kx", "ky", "kz", None, None),
        P("kx", "ky", "kz", None),
    )
    sizes = tuple(mesh.shape[a] for a in ("kx", "ky", "kz"))
    return jax.shard_map(
        functools.partial(per_device, sizes),
        mesh=mesh,
        in_specs=placed,
        out_specs=P("kx", None, None, "ky", "kz"),
        check_vma=False,
    )
```

```python
import functools
import jax
import jax.numpy as jnp
from jax import lax
from jax.experimental import pallas as pl
from jax.experimental.pallas import tpu as pltpu
from jax.sharding import PartitionSpec as P

ITERS = 2
MESH = pl.DeviceIdType.MESH
LANES = 128


def roll(v, by):
    by = by % LANES
    return v if by == 0 else pltpu.roll(v, by, axis=1)


def main_kernel(sizes, pop, force, rate, tiles, send_hbm, target_hbm, tile_hbm, count_hbm, out,
                send_planes, recv_target, recv_tile, recv_count, pop_in, force_in, rate_in, tiles_in, ext, mid, field, base, y_out, y_in, z_out, z_in,
                p_out, p_in, in_sem, pop_sem, tile_sem, x_send, x_recv, y_send, y_recv, z_send, z_recv, p_send, p_recv):
    n_x, n_y, n_z, wx, drives, bands, wy, wz, cap, n_tiles = sizes
    rows = bands * wy
    length = rows * wz
    pieces = length // LANES
    per = LANES // wz
    halves = wy // per
    chunks = p_in.shape[1]
    wide = length // chunks
    mx, my, mz = lax.axis_index("kx"), lax.axis_index("ky"), lax.axis_index("kz")

    def around(me, size, by):
        return lax.rem(me + (by % size), size)

    barrier = pltpu.get_barrier_semaphore()
    friends = []
    for name, me, size, offsets in (("kx", mx, n_x, {1, n_x - 1}), ("ky", my, n_y, {1, n_y - 1}), ("kz", mz, n_z, set(range(1, n_z)))):
        for by in sorted(offsets):
            friends.append({name: around(me, size, by)})
    for friend in friends:
        pl.semaphore_signal(barrier, inc=1, device_id=friend, device_id_type=MESH)

    pop_rows = drives * rows
    pop_loads = [pltpu.make_async_copy(pop.at[pl.ds(x * pop_rows, pop_rows)], pop_in.at[pl.ds(x * pop_rows, pop_rows)], pop_sem.at[x])
                 for x in range(wx)]
    for load in pop_loads:
        load.start()
    pairs = ((send_hbm, send_planes), (target_hbm, recv_target), (tile_hbm, recv_tile), (count_hbm, recv_count), (force, force_in), (rate, rate_in))
    loads = [pltpu.make_async_copy(a, b, in_sem.at[i]) for i, (a, b) in enumerate(pairs)]
    for load in loads:
        load.start()
    tile_loads = [pltpu.make_async_copy(tiles.at[t], tiles_in.at[t], tile_sem.at[t]) for t in range(n_tiles)]

    lane = lax.broadcasted_iota(jnp.int32, (8, LANES), 1)
    z_of = lax.rem(lane, wz)

    for x in range(wx):
        pop_loads[x].wait()
        for v in range(pieces):
            piece = jnp.concatenate(
                [pop_in[pl.ds(x * pop_rows + v * per + i, drives, stride=rows), :] for i in range(per)], axis=1)
            ext[0, x + 2, :, v * LANES:(v + 1) * LANES] = piece
            mid[x, :, v * LANES:(v + 1) * LANES] = piece
    for load in tile_loads:
        load.start()
    loads[0].wait()
    pl.semaphore_wait(barrier, len(friends))

    sel = None
    in_flight = []
    for it in range(ITERS):
        cur = ext.at[it]
        waits_p = [[] for _ in range(chunks)]
        for k in range(n_z - 1, -1, -1):
            peer = around(mz, n_z, k)
            blocks = jnp.concatenate(
                [mid[send_planes[0, 0, 0, c, peer]] for c in range(cap)], axis=0).astype(jnp.bfloat16)
            part = pl.ds(k * cap * drives, cap * drives)
            for q in range(chunks):
                piece = blocks[:, q * wide:(q + 1) * wide]
                if k == 0:
                    p_in[it, q, 0:cap * drives, :] = piece
                else:
                    p_out[it, q, k * cap * drives:(k + 1) * cap * drives, :] = piece
                    waits_p[q].append(pltpu.make_async_remote_copy(
                        p_out.at[it, q, part], p_in.at[it, q, part], p_send.at[it, q, k], p_recv.at[it, q, k],
                        device_id={"kz": peer}, device_id_type=MESH))
        early = (chunks + 1) // 2
        for q in range(early):
            for copy in waits_p[q]:
                copy.start()
        waits_h = [
            pltpu.make_async_remote_copy(
                cur.at[wx:wx + 2], cur.at[0:2], x_send.at[it, 0], x_recv.at[it, 0],
                device_id={"kx": around(mx, n_x, 1)}, device_id_type=MESH),
            pltpu.make_async_remote_copy(
                cur.at[2:4], cur.at[wx + 2:wx + 4], x_send.at[it, 1], x_recv.at[it, 1],
                device_id={"kx": around(mx, n_x, -1)}, device_id_type=MESH)]
        for copy in waits_h:
            copy.start()

        width = 2 * wz
        for x0 in range(0, wx, 2):
            ups, downs = [], []
            for x in (x0, x0 + 1):
                part = [cur[x + 2, :, v * LANES:(v + 1) * LANES] for v in range(pieces)]
                up_z = jnp.zeros((drives, LANES), jnp.float32)
                down_z = up_z
                for v in range(pieces):
                    c = part[v]
                    last = jnp.where(z_of == wz - 2, c - 8.0 * roll(c, -1), c)
                    first = jnp.where(z_of == 0, -c, 8.0 * roll(c, 1) - c)
                    here = lax.div(z_of, 2) == v
                    up_z = jnp.where(here, roll(last, 2 * v - (wz - 2)), up_z)
                    down_z = jnp.where(here, roll(first, 2 * v), down_z)
                ups.append(up_z)
                downs.append(down_z)
                up_y = jnp.zeros((drives, LANES), jnp.float32)
                down_y = up_y
                for b in range(bands):
                    here = lax.div(lane, width) == b
                    up_y = jnp.where(here, roll(part[b * halves + halves - 1], width * b - (LANES - width)), up_y)
                    down_y = jnp.where(here, roll(part[b * halves], width * b), down_y)
                y_out[it, 0, x] = up_y
                y_out[it, 1, x] = down_y
            z_out[it, 0, x0 * drives:(x0 + 2) * drives] = jnp.concatenate(ups, axis=0).astype(jnp.bfloat16)
            z_out[it, 1, x0 * drives:(x0 + 2) * drives] = jnp.concatenate(downs, axis=0).astype(jnp.bfloat16)

        for name, me, size, o, i, ss, rs in (("kz", mz, n_z, z_out, z_in, z_send, z_recv), ("ky", my, n_y, y_out, y_in, y_send, y_recv)):
            for way in range(2):
                copy = pltpu.make_async_remote_copy(
                    o.at[it, way], i.at[it, way], ss.at[it, way], rs.at[it, way],
                    device_id={name: around(me, size, 1 if way == 0 else -1)}, device_id_type=MESH)
                copy.start()
                waits_h.append(copy)
        for q in range(early, chunks):
            for copy in waits_p[q]:
                copy.start()

        if it == 0:
            for load in loads[1:]:
                load.wait()
            for v in range(pieces):
                at = slice(v * LANES, (v + 1) * LANES)
                for a in range(4):
                    source, first, stride = (force_in, a * rows, 3 * rows) if a < 3 else (rate_in, 0, rows)
                    piece = jnp.concatenate(
                        [source[pl.ds(first + v * per + i, wx, stride=stride), :] for i in range(per)], axis=1)
                    if a < 3:
                        piece = piece * (1.0 / 12.0)
                    for x in range(wx):
                        field[a, x, :, at] = jnp.broadcast_to(piece[x:x + 1], (drives, LANES))
            slots = n_z * cap
            col = lax.broadcasted_iota(jnp.int32, (8, slots * drives), 1)
            pair = jnp.full((8, slots * drives), -1, jnp.int32)
            for k in range(n_z):
                source = around(mz, n_z, -k)
                count = recv_count[0, 0, 0, source]
                for c in range(cap):
                    code = jnp.where(c < count, recv_tile[0, 0, 0, c, source] * wx + recv_target[0, 0, 0, c, source], -1)
                    pair = jnp.where(lax.div(col, drives) == k * cap + c, code, pair)
            row = lax.broadcasted_iota(jnp.int32, (n_tiles * wx * drives, slots * drives), 0)
            col = lax.broadcasted_iota(jnp.int32, (n_tiles * wx * drives, slots * drives), 1)
            hit = (lax.div(row, drives) == pair[0:1]) & (lax.rem(row, drives) == lax.rem(col, drives))
            sel = jnp.where(hit, 1.0, 0.0).astype(jnp.bfloat16)

        for copy in waits_h:
            copy.wait_recv()

        def step(pair_at, carry):
            both = pl.ds(pl.multiple_of(pair_at * 2 * drives, 2 * drives), 2 * drives)
            zps, zns = z_in[it, 0, both].astype(jnp.float32), z_in[it, 1, both].astype(jnp.float32)
            for j in range(2):
                x = pair_at * 2 + j
                zp, zn = zps[j * drives:(j + 1) * drives], zns[j * drives:(j + 1) * drives]
                yp, yn = y_in[it, 0, x], y_in[it, 1, x]
                part = [cur[x + 2, :, v * LANES:(v + 1) * LANES] for v in range(pieces)]
                for v in range(pieces):
                    at = slice(v * LANES, (v + 1) * LANES)
                    b, h = divmod(v, halves)
                    c = part[v]
                    dx = 8.0 * (cur[x + 3, :, at] - cur[x + 1, :, at]) - (cur[x + 4, :, at] - cur[x, :, at])
                    after = part[v + 1] if h < halves - 1 else roll(yn, -width * b)
                    before = part[v - 1] if h > 0 else roll(yp, LANES - width - width * b)
                    y1 = roll(jnp.where(lane < wz, after, c), -wz)
                    y2 = roll(jnp.where(lane < 2 * wz, after, c), -2 * wz)
                    w1 = roll(jnp.where(lane >= LANES - wz, before, c), wz)
                    w2 = roll(jnp.where(lane >= LANES - 2 * wz, before, c), 2 * wz)
                    dy = 8.0 * (y1 - w1) - (y2 - w2)
                    a1 = jnp.where(z_of < wz - 1, roll(c, -1), 0.0)
                    b1 = jnp.where(z_of >= 1, roll(c, 1), 0.0)
                    a2 = jnp.where(z_of < wz - 2, roll(c, -2), 0.0)
                    b2 = jnp.where(z_of >= 2, roll(c, 2), 0.0)
                    edge = jnp.where(z_of < 2, roll(zp, -2 * v), jnp.where(z_of >= wz - 2, roll(zn, wz - 2 - 2 * v), 0.0))
                    dz = 8.0 * (a1 - b1) - (a2 - b2) + edge
                    fx, fy, fz, r = (field[a, x, :, at] for a in range(4))
                    base[pl.ds(pl.multiple_of(x * drives, drives), drives), at] = c - (fx * dx + fy * dy + fz * dz) - r * c
            return carry

        lax.fori_loop(0, wx // 2, step, 0)

        m = wx * drives
        total = base[...]
        for q in range(chunks):
            for copy in waits_p[q]:
                copy.wait_recv()
            grouped = jnp.dot(sel, p_in[it, q], preferred_element_type=jnp.float32).astype(jnp.bfloat16)
            for t in range(n_tiles):
                if it == 0 and q == 0:
                    tile_loads[t].wait()
                total = total + lax.dot_general(
                    grouped[t * m:(t + 1) * m], tiles_in[t, :, q * wide:(q + 1) * wide],
                    (((1,), (1,)), ((), ())), preferred_element_type=jnp.float32)
        total = total.reshape(wx, drives, length)
        if it == ITERS - 1:
            out[...] = total
        else:
            ext[it + 1, 2:wx + 2] = total
            mid[...] = total
        in_flight += sum(waits_p, []) + waits_h
    for copy in in_flight:
        copy.wait_send()


def spread_kernel(sizes, dense_hbm, out, dense, laid, in_sem, sem):
    wx, drives, rows, wz = sizes
    per = LANES // wz
    pieces = rows // per
    loads = [pltpu.make_async_copy(dense_hbm.at[x], dense.at[x], in_sem.at[x]) for x in range(wx)]
    for load in loads:
        load.start()
    copies = []
    for x in range(wx):
        loads[x].wait()
        for v in range(pieces):
            piece = dense[x, :, v * LANES:(v + 1) * LANES]
            for i in range(per):
                laid[pl.ds(x * drives * rows + v * per + i, drives, stride=rows), :] = roll(piece, -i * wz)[:, :wz]
        part = pl.ds(x * drives * rows, drives * rows)
        copies.append(pltpu.make_async_copy(laid.at[part], out.at[part], sem.at[x]))
        copies[-1].start()
    for copy in copies:
        copy.wait()


def per_device(mesh_shape, populations, force, rate, tiles, send_planes, recv_target, recv_tile, recv_count):
    wx, drives, bands, wy, wz = populations.shape
    cap = send_planes.shape[-1]
    n_tiles, length, _ = tiles.shape
    n_x, n_y, n_z = mesh_shape
    rows = bands * wy
    sizes = (n_x, n_y, n_z, wx, drives, bands, wy, wz, cap, n_tiles)
    vmem = pl.BlockSpec(memory_space=pltpu.VMEM)
    chunks = 2 if n_z <= 8 else 1
    hbm = pl.BlockSpec(memory_space=pltpu.HBM)
    f32, b16 = jnp.float32, jnp.bfloat16
    dma = pltpu.SemaphoreType.DMA
    dense = pl.pallas_call(
        functools.partial(main_kernel, sizes),
        out_shape=jax.ShapeDtypeStruct((wx, drives, length), f32),
        in_specs=[hbm] * 8,
        out_specs=vmem,
        scratch_shapes=[
            pltpu.SMEM((1, 1, 1, cap, n_z), jnp.int32),
            pltpu.SMEM((1, 1, 1, cap, n_z), jnp.int32),
            pltpu.SMEM((1, 1, 1, cap, n_z), jnp.int32),
            pltpu.SMEM((1, 1, 1, n_z), jnp.int32),
            pltpu.VMEM((wx * drives * rows, wz), f32),
            pltpu.VMEM((wx * 3 * rows, wz), f32),
            pltpu.VMEM((wx * rows, wz), f32),
            pltpu.VMEM(tiles.shape, b16),
            pltpu.VMEM((ITERS, wx + 4, drives, length), f32),
            pltpu.VMEM((wx, drives, length), f32),
            pltpu.VMEM((4, wx, drives, length), f32),
            pltpu.VMEM((wx * drives, length), f32),
            pltpu.VMEM((ITERS, 2, wx, drives, LANES), f32),
            pltpu.VMEM((ITERS, 2, wx, drives, LANES), f32),
            pltpu.VMEM((ITERS, 2, wx * drives, LANES), b16),
            pltpu.VMEM((ITERS, 2, wx * drives, LANES), b16),
            pltpu.VMEM((ITERS, chunks, n_z * cap * drives, length // chunks), b16),
            pltpu.VMEM((ITERS, chunks, n_z * cap * drives, length // chunks), b16),
            dma((6,)), dma((wx,)), dma((n_tiles,)),
            dma((ITERS, 2)), dma((ITERS, 2)), dma((ITERS, 2)), dma((ITERS, 2)), dma((ITERS, 2)), dma((ITERS, 2)),
            dma((ITERS, chunks, n_z)), dma((ITERS, chunks, n_z)),
        ],
        compiler_params=pltpu.CompilerParams(collective_id=0, has_side_effects=True, vmem_limit_bytes=60 * 2**20),
        name="steps",
    )(
        populations.reshape(wx * drives * rows, wz),
        force.reshape(wx * 3 * rows, wz),
        rate.reshape(wx * rows, wz),
        tiles,
        jnp.swapaxes(send_planes, -1, -2),
        jnp.swapaxes(recv_target, -1, -2),
        jnp.swapaxes(recv_tile, -1, -2),
        recv_count,
    )
    spread = pl.pallas_call(
        functools.partial(spread_kernel, (wx, drives, rows, wz)),
        out_shape=jax.ShapeDtypeStruct((wx * drives * rows, wz), f32),
        in_specs=[hbm],
        out_specs=hbm,
        scratch_shapes=[pltpu.VMEM((wx, drives, length), f32), pltpu.VMEM((wx * drives * rows, wz), f32), dma((wx,)), dma((wx,))],
        compiler_params=pltpu.CompilerParams(vmem_limit_bytes=60 * 2**20),
        name="spread",
    )(dense)
    return spread.reshape(populations.shape)


def solution(mesh):
    placed = (
        P("kx", None, None, "ky", "kz"),
        P("kx", None, None, "ky", "kz"),
        P("kx", None, "ky", "kz"),
        P(),
        P("kx", "ky", "kz", None, None),
        P("kx", "ky", "kz", None, None),
        P("kx", "ky", "kz", None, None),
        P("kx", "ky", "kz", None),
    )
    sizes = tuple(mesh.shape[a] for a in ("kx", "ky", "kz"))
    return jax.shard_map(
        functools.partial(per_device, sizes),
        mesh=mesh,
        in_specs=placed,
        out_specs=P("kx", None, None, "ky", "kz"),
        check_vma=False,
    )
```
